32 devices in a mesh: grp: 2 (over x), col: 8 (over z, y), row: 2 (over core).
Axes of the slice: x: 2, y: 2, z: 4, core: 2. Of those that a mesh axis runs over, the one named last changes fastest.
Arguments:
- cost: float32 [32, 8, 4096], P('grp', 'col', 'row'), parts along dimension 0, may hold values from -6 to 6
- rhs: float32 [32, 2, 16384], P('grp', 'row', 'col'), parts along dimension 0, may hold values from -6 to 6
- primal: float32 [32, 8, 4096], P('grp', 'col', 'row'), parts along dimension 0, may hold values from 0 to 1
- dual: float32 [32, 2, 16384], P('grp', 'row', 'col'), parts along dimension 0, may hold values from 0 to 1
- bound_kind: int32 [16, 4096], P(('grp', 'col'), 'row'), parts along dimension 0, may hold values from 0 to 2
- upper: float32 [16, 4096], P(('grp', 'col'), 'row'), parts along dimension 0, may hold values from 0.3 to 3
- kblocks: bfloat16 [16, 2, 256, 128, 128], P(('grp', 'col'), 'row'), parts along dimension 0, may hold values from -0.125 to 0.125
- block_row: int32 [16, 2, 256], P(('grp', 'col'), 'row'), parts along dimension 0, may hold values from 0 to 127
- block_col: int32 [16, 2, 256], P(('grp', 'col'), 'row'), parts along dimension 0, may hold values from 0 to 31
- block_count: int32 [16, 2], P(('grp', 'col'), 'row'), parts along dimension 0, may hold values from 32 to 256, as said below
Outputs:
- primal_out: float32 [32, 8, 4096], P('grp', 'col', 'row'), parts along dimension 0
- dual_out: float32 [32, 2, 16384], P('grp', 'row', 'col'), parts along dimension 0
The draws below stay inside these ranges and needn't reach their ends.
There are 2 independent parts, one for each index of `grp`. The reference program is written for one: setup_inputs(seed, part) draws one part's arguments, and reference() takes and returns one part's arrays. A program takes and returns all parts, laid end to end along the dimension named above; each array names one. Nothing has to cross between parts.
Inputs may be any that keep to these rules, and one draw needn't show every extreme that they name: `block_count`: equals 256 for at least one tile of every part. `block_row`: live slots of one tile may name the same block position.
All inputs are finite; a program needn't handle non-finite values.
Results may differ from the reference program's by a relative error of at most 0.003.
Values may be sent and summed in bfloat16 or wider, within the bound.
No kernel may reach another device: no remote copies, remote signals or barrier semaphores. Data moves between devices by JAX's collectives and lax.ppermute only.
A program may use at most 64 MiB of HBM per device.

```python
import math
import jax
import jax.numpy as jnp
from jax import lax

SCEN = 16
BS = 128
COLB_DEV = 32
ROWB_DEV = 128
NB_DEV = 256
ITERS = 6
COL_SLAB = 4096
ROW_SLAB = 16384
N_COL = 8
N_ROW = 2


def draw_block_count(key, part):
    key = jax.random.fold_in(key, 7)
    first, second = jax.random.split(key)
    counts = jax.random.randint(first, (N_COL * N_ROW,), max(NB_DEV // 8, 1), NB_DEV + 1)
    place = jax.random.randint(second, (), 0, N_COL * N_ROW)
    counts = jnp.where(jnp.arange(N_COL * N_ROW) == place, NB_DEV, counts)
    return counts.reshape(N_COL, N_ROW).astype(jnp.int32)


def touch_ends(entries, key, least, largest):
    index_at = [jax.random.randint(jax.random.fold_in(key, axis), (), 0, length) for axis, length in enumerate(entries.shape)]
    widest = entries.shape.index(max(entries.shape))
    neighbour = index_at[:widest] + [(index_at[widest] + 1) % entries.shape[widest]] + index_at[widest + 1:]
    return entries.at[tuple(index_at)].set(least).at[tuple(neighbour)].set(largest)


def block_scale(key, dims, shards, least, high):
    factor_of = 1.0
    for position, shards_of in shards:
        draws = jax.random.uniform(jax.random.fold_in(jax.random.fold_in(key, 6), position), (shards_of,), jnp.float32, least / len(shards), high / len(shards))
        factor_of = factor_of * jnp.repeat(jnp.exp(draws), dims[position] // shards_of).reshape((-1,) + (1,) * (len(dims) - 1 - position))
    return factor_of


def bell_draw(stream_key, dims, width, most, cuts=(), kind=jnp.bfloat16):
    factor_of = block_scale(stream_key, dims, cuts, -0.22, 0.18) if cuts else 1.0
    result = jax.random.normal(stream_key, dims, jnp.float32) * width * factor_of
    return jnp.minimum(jnp.maximum(result, -most), most).astype(kind)


def setup_inputs(seed: int = 0, part: int = 0) -> dict:
    key_list = jax.random.split(jax.random.key(seed), 11)
    own_keys = jax.random.split(jax.random.fold_in(key_list[10], part), 11)
    return {
        "cost": bell_draw(own_keys[0], (SCEN, N_COL, COL_SLAB), 1.0, 6.0, ((1, 8), (2, 2)), jnp.float32),
        "rhs": bell_draw(own_keys[1], (SCEN, N_ROW, ROW_SLAB), 1.0, 6.0, ((1, 2), (2, 8)), jnp.float32),
        "primal": jnp.clip(1.0 * jax.random.uniform(own_keys[2], (SCEN, N_COL, COL_SLAB), jnp.float32) ** block_scale(own_keys[2], (SCEN, N_COL, COL_SLAB), ((1, 8), (2, 2)), -0.2, 0.2), 0.0, 1.0),
        "dual": jnp.clip(1.0 * jax.random.uniform(own_keys[3], (SCEN, N_ROW, ROW_SLAB), jnp.float32) ** block_scale(own_keys[3], (SCEN, N_ROW, ROW_SLAB), ((1, 2), (2, 8)), -0.2, 0.2), 0.0, 1.0),
        "bound_kind": touch_ends(jax.random.randint(own_keys[4], (N_COL, COL_SLAB), 0, 3), jax.random.fold_in(own_keys[4], 1), 0, 2).astype(jnp.int32),
        "upper": jnp.clip(jnp.exp(math.log(3.0) - 2.3025851 * jax.random.uniform(own_keys[5], (N_COL, COL_SLAB), jnp.float32) ** block_scale(own_keys[5], (N_COL, COL_SLAB), ((0, 8), (1, 2)), -0.2, 0.2)), 0.3, 3.0),
        "kblocks": bell_draw(own_keys[6], (N_COL, N_ROW, NB_DEV, BS, BS), (BS * NB_DEV * N_COL // ROWB_DEV) ** -0.5, 0.125, ((0, 8), (1, 2))),
        "block_row": touch_ends(jax.random.randint(own_keys[7], (N_COL, N_ROW, NB_DEV), 0, ROWB_DEV), jax.random.fold_in(own_keys[7], 1), 0, ROWB_DEV - 1).astype(jnp.int32),
        "block_col": touch_ends(jax.random.randint(own_keys[8], (N_COL, N_ROW, NB_DEV), 0, COLB_DEV), jax.random.fold_in(own_keys[8], 1), 0, COLB_DEV - 1).astype(jnp.int32),
        "block_count": draw_block_count(jax.random.fold_in(jax.random.fold_in(key_list[10], part), 71), part),
    }


def forward_tile(kb, brow, bcol, live, xs):
    picked = jnp.take(xs.reshape(xs.shape[0], -1, BS), bcol, axis=1)
    prod = jnp.einsum('nij,snj->nsi', kb.astype(jnp.float32), picked.astype(jnp.float32))
    prod = prod * live[:, None, None]
    summed = jax.ops.segment_sum(prod, brow, num_segments=ROWB_DEV)
    return jnp.transpose(summed, (1, 0, 2)).reshape(xs.shape[0], ROWB_DEV * BS)

def backward_tile(kb, brow, bcol, live, ys):
    picked = jnp.take(ys.reshape(ys.shape[0], -1, BS), brow, axis=1)
    prod = jnp.einsum('nij,sni->nsj', kb.astype(jnp.float32), picked.astype(jnp.float32))
    prod = prod * live[:, None, None]
    summed = jax.ops.segment_sum(prod, bcol, num_segments=COLB_DEV)
    return jnp.transpose(summed, (1, 0, 2)).reshape(ys.shape[0], COLB_DEV * BS)

def project(value, kind, upper):
    lifted = jnp.where(kind == 2, value, jnp.maximum(value, 0.0))
    return jnp.where(kind == 1, jnp.minimum(lifted, upper), lifted)

def reference(cost, rhs, primal, dual, bound_kind, upper, kblocks, block_row, block_col, block_count):
    slots = jnp.arange(NB_DEV, dtype=jnp.int32)
    live_all = (slots[None, None, :] < block_count[:, :, None]).astype(jnp.float32)
    x_state = primal
    y_state = dual
    for step in range(ITERS):
        y_half = y_state.astype(jnp.bfloat16)

        def column_grad(index):
            total = jnp.zeros((SCEN, COLB_DEV * BS), jnp.float32)
            for rank in range(N_ROW):
                total = total + backward_tile(kblocks[index, rank], block_row[index, rank], block_col[index, rank], live_all[index, rank], y_half[:, rank])
            return total
        grad = jnp.transpose(lax.map(column_grad, jnp.arange(N_COL, dtype=jnp.int32)), (1, 0, 2))
        x_next = project(x_state - 0.4 * (cost - grad), bound_kind[None], upper[None])
        x_bar = (2.0 * x_next - x_state).astype(jnp.bfloat16)

        def add_rows(carry, index):
            parts = []
            for rank in range(N_ROW):
                parts.append(forward_tile(kblocks[index, rank], block_row[index, rank], block_col[index, rank], live_all[index, rank], x_bar[:, index]))
            return (carry + jnp.stack(parts, axis=1), None)
        start = jnp.zeros((SCEN, N_ROW, ROWB_DEV * BS), jnp.float32)
        image, _ = lax.scan(add_rows, start, jnp.arange(N_COL, dtype=jnp.int32))
        y_state = jnp.maximum(0.0, y_state + 0.9 * (rhs - image))
        x_state = x_next
    return (x_state, y_state)
```

```python
import functools

import jax
import jax.numpy as jnp
from jax import lax
from jax.experimental import pallas as pl
from jax.experimental.pallas import tpu as pltpu
from jax.sharding import PartitionSpec as P

BS = 128
ITERS = 6
UNROLL = 32
NN = (((1,), (0,)), ((), ()))
NT = (((1,), (1,)), ((), ()))

SMEM = pl.BlockSpec(memory_space=pltpu.SMEM)
VMEM = pl.BlockSpec(memory_space=pltpu.VMEM)
PARAMS = pltpu.CompilerParams(vmem_limit_bytes=24 * 2**20)


def products(groups, src, dst, vecs, blocks, acc, dims):
    def group(g, _):
        first = g * UNROLL
        terms = [
            lax.dot_general(vecs[src[first + u]], blocks[first + u], dims, preferred_element_type=jnp.float32)
            for u in range(UNROLL)
        ]
        for u in range(UNROLL):
            acc[dst[first + u]] += terms[u]
        return 0

    lax.fori_loop(0, groups, group, 0)


def backward_kernel(n_pieces, groups, src, dst, blocks, *refs):
    pieces, (grad, vecs, acc) = refs[:n_pieces], refs[n_pieces:]
    span = pieces[0].shape[0]
    for m in range(n_pieces):
        vecs[pl.ds(m * span, span)] = pieces[m][...]
    acc[...] = jnp.zeros(acc.shape, acc.dtype)
    products(groups[0], src, dst, vecs, blocks, acc, NN)
    grad[...] = acc[pl.ds(0, grad.shape[0])]


def forward_kernel(n_pieces, groups, src, dst, blocks, own, other, x_ref, cost, kind, upper, *refs):
    x_out, pieces, (vecs, acc) = refs[0], refs[1 : 1 + n_pieces], refs[1 + n_pieces :]
    x = x_ref[...]
    value = x - 0.4 * (cost[...] - (own[...] + other[...]))
    lifted = jnp.where(kind[...] == 2, value, jnp.maximum(value, 0.0))
    x_next = jnp.where(kind[...] == 1, jnp.minimum(lifted, upper[...]), lifted)
    x_out[...] = x_next
    vecs[...] = (2.0 * x_next - x).astype(vecs.dtype)
    acc[...] = jnp.zeros(acc.shape, acc.dtype)
    products(groups[0], src, dst, vecs, blocks, acc, NT)
    span = pieces[0].shape[0]
    for m in range(n_pieces):
        pieces[m][...] = acc[pl.ds(m * span, span)].astype(pieces[m].dtype)


def dual_kernel(n_pieces, y_ref, rhs, *refs):
    pieces, (y_out, y_half) = refs[:n_pieces], refs[n_pieces:]
    image = pieces[0][...]
    for m in range(1, n_pieces):
        image = image + pieces[m][...].astype(jnp.float32)
    y = jnp.maximum(0.0, y_ref[...] + 0.9 * (rhs[...] - image))
    y_out[...] = y
    y_half[...] = y.astype(y_half.dtype)


def to_blocks(a):
    return jnp.transpose(a.reshape(a.shape[0], -1, BS), (1, 0, 2))


def from_blocks(a):
    return jnp.transpose(a, (1, 0, 2)).reshape(a.shape[1], -1)


def per_device(
    cost, rhs, primal, dual, bound_kind, upper, kblocks, block_row, block_col, block_count
):
    n_col = lax.axis_size("col")
    n_row = lax.axis_size("row")
    scen = primal.shape[0]
    own_cols, own_rows = primal.shape[2], dual.shape[2]
    span = own_rows // BS
    col_blocks = own_cols * n_row // BS
    row_blocks = span * n_col
    direct = n_col <= 8 and n_col & (n_col - 1) == 0 and span & (span - 1) == 0
    n_pieces = n_col if direct else 1

    tile = kblocks[0, 0]
    slots = jnp.arange(tile.shape[0], dtype=jnp.int32)
    count = block_count[0, 0]
    live = slots < count
    groups = ((count + UNROLL - 1) // UNROLL).reshape(1)
    brow, bcol = block_row[0, 0], block_col[0, 0]
    if direct:
        brow = brow ^ (lax.axis_index("col") * span)
    to_col = jnp.where(live, bcol, col_blocks)
    to_row = jnp.where(live, brow, row_blocks)

    def swap(a):
        return lax.ppermute(a, "row", [(i, n_row - 1 - i) for i in range(n_row)])

    def whole(a):
        return lax.all_gather(a, "row", axis=0, tiled=True)

    x = whole(to_blocks(primal[:, 0]))
    cost_all = whole(to_blocks(cost[:, 0]))
    kind_all = whole(to_blocks(bound_kind))
    upper_all = whole(to_blocks(upper))
    y = to_blocks(dual[:, 0])
    rhs_own = to_blocks(rhs[:, 0])

    def partner(a, m):
        return lax.ppermute(a, "col", [(i, i ^ m) for i in range(n_col)])

    x_shape = jax.ShapeDtypeStruct(x.shape, jnp.float32)
    y_shape = jax.ShapeDtypeStruct(y.shape, jnp.float32)
    y_half_shape = jax.ShapeDtypeStruct(y.shape, jnp.bfloat16)
    if direct:
        piece_shapes = (y_shape,) + (y_half_shape,) * (n_pieces - 1)
    else:
        piece_shapes = (jax.ShapeDtypeStruct((row_blocks, scen, BS), jnp.float32),)

    backward = pl.pallas_call(
        functools.partial(backward_kernel, n_pieces),
        out_shape=x_shape,
        in_specs=[SMEM] * 3 + [VMEM] * (1 + n_pieces),
        out_specs=VMEM,
        scratch_shapes=[
            pltpu.VMEM((row_blocks, scen, BS), jnp.bfloat16),
            pltpu.VMEM((col_blocks + 1, scen, BS), jnp.float32),
        ],
        compiler_params=PARAMS,
        name="backward",
    )
    forward = pl.pallas_call(
        functools.partial(forward_kernel, n_pieces),
        out_shape=(x_shape,) + piece_shapes,
        in_specs=[SMEM] * 3 + [VMEM] * 7,
        out_specs=(VMEM,) * (1 + n_pieces),
        scratch_shapes=[
            pltpu.VMEM((col_blocks, scen, BS), jnp.bfloat16),
            pltpu.VMEM((row_blocks + 1, scen, BS), jnp.float32),
        ],
        compiler_params=PARAMS,
        name="forward",
    )
    dual_step = pl.pallas_call(
        functools.partial(dual_kernel, n_pieces),
        out_shape=(y_shape, y_half_shape),
        in_specs=[VMEM] * (2 + n_pieces),
        out_specs=(VMEM, VMEM),
        compiler_params=PARAMS,
        name="dual_step",
    )

    y_half = y.astype(jnp.bfloat16)
    for step in range(ITERS):
        if direct:
            y_slab = [y_half] + [partner(y_half, m) for m in range(1, n_col)]
        else:
            y_slab = [lax.all_gather(y_half, "col", axis=0, tiled=True)]
        grad = backward(groups, brow, to_col, tile, *y_slab)
        x, *pieces = forward(groups, bcol, to_row, tile, grad, swap(grad), x, cost_all, kind_all, upper_all)
        if direct:
            image = pieces[:1] + [partner(pieces[m], m) for m in range(1, n_col)]
        else:
            image = [lax.psum_scatter(pieces[0], "col", scatter_dimension=0, tiled=True)]
        y, y_half = dual_step(y, rhs_own, *image)

    here = lax.axis_index("row") * (own_cols // BS)
    x_own = lax.dynamic_slice_in_dim(x, here, own_cols // BS, axis=0)
    return (from_blocks(x_own)[:, None, :], from_blocks(y)[:, None, :])


def solution(mesh):
    return jax.shard_map(
        per_device,
        mesh=mesh,
        in_specs=(
            P("grp", "col", "row"),
            P("grp", "row", "col"),
            P("grp", "col", "row"),
            P("grp", "row", "col"),
            P(("grp", "col"), "row"),
            P(("grp", "col"), "row"),
            P(("grp", "col"), "row", None, None, None),
            P(("grp", "col"), "row", None),
            P(("grp", "col"), "row", None),
            P(("grp", "col"), "row"),
        ),
        out_specs=(P("grp", "col", "row"), P("grp", "row", "col")),
        check_vma=False,
    )
```

```python
import functools

import jax
import jax.numpy as jnp
from jax import lax
from jax.experimental import pallas as pl
from jax.experimental.pallas import tpu as pltpu
from jax.sharding import PartitionSpec as P

BS = 128
ITERS = 6
UNROLL = 32
NN = (((1,), (0,)), ((), ()))
NT = (((1,), (1,)), ((), ()))

SMEM = pl.BlockSpec(memory_space=pltpu.SMEM)
VMEM = pl.BlockSpec(memory_space=pltpu.VMEM)
PARAMS = pltpu.CompilerParams(vmem_limit_bytes=24 * 2**20)


def products(groups, src, dst, vecs, blocks, acc, dims):
    def group(g, _):
        first = g * UNROLL
        terms = [
            lax.dot_general(vecs[src[first + u]], blocks[first + u], dims, preferred_element_type=jnp.float32)
            for u in range(UNROLL)
        ]
        for u in range(UNROLL):
            acc[dst[first + u]] += terms[u]
        return 0

    lax.fori_loop(0, groups, group, 0)


def backward_kernel(groups, src, dst, blocks, *refs):
    pieces, (grad, vecs, acc) = refs[:-3], refs[-3:]
    half = len(pieces)
    span = pieces[0].shape[0] // 2
    for m in range(half):
        vecs[pl.ds(m * span, span)] = pieces[m][pl.ds(0, span)]
        vecs[pl.ds((m + half) * span, span)] = pieces[m][pl.ds(span, span)]
    acc[...] = jnp.zeros(acc.shape, acc.dtype)
    products(groups[0], src, dst, vecs, blocks, acc, NN)
    grad[...] = acc[pl.ds(0, grad.shape[0])]


def whole_backward_kernel(groups, src, dst, blocks, vecs, grad, acc):
    acc[...] = jnp.zeros(acc.shape, acc.dtype)
    products(groups[0], src, dst, vecs, blocks, acc, NN)
    grad[...] = acc[pl.ds(0, grad.shape[0])]


def forward_kernel(groups, src, dst, blocks, own, other, x_ref, cost, kind, upper, *refs):
    x_out, pieces, (vecs, acc) = refs[0], refs[1:-2], refs[-2:]
    cols = x_ref.shape[0] // 2
    for h in range(2):
        here, there = pl.ds(h * cols, cols), pl.ds((1 - h) * cols, cols)
        x = x_ref[here]
        value = x - 0.4 * (cost[here] - (own[here] + other[there]))
        lifted = jnp.where(kind[here] == 2, value, jnp.maximum(value, 0.0))
        x_next = jnp.where(kind[here] == 1, jnp.minimum(lifted, upper[here]), lifted)
        x_out[here] = x_next
        vecs[here] = (2.0 * x_next - x).astype(vecs.dtype)
    acc[...] = jnp.zeros(acc.shape, acc.dtype)
    products(groups[0], src, dst, vecs, blocks, acc, NT)
    half = len(pieces)
    span = pieces[0].shape[0] // 2
    for m in range(half):
        pieces[m][pl.ds(0, span)] = acc[pl.ds(m * span, span)].astype(pieces[m].dtype)
        pieces[m][pl.ds(span, span)] = acc[pl.ds((m + half) * span, span)].astype(pieces[m].dtype)


def near_sum_kernel(own, *refs):
    pieces, (total, sent) = refs[:-2], refs[-2:]
    image = own[...]
    for piece in pieces:
        image = image + piece[...].astype(jnp.float32)
    total[...] = image
    n = sent.shape[0]
    sent[...] = image[image.shape[0] - n :].astype(sent.dtype)


def dual_kernel(y_ref, rhs, near, far, y_out, y_half):
    span = near.shape[0] // 2
    for h in range(y_out.shape[0] // span):
        here = pl.ds(h * span, span)
        there = pl.ds(far.shape[0] - (h + 1) * span, span)
        image = near[here] + far[there].astype(jnp.float32)
        y = jnp.maximum(0.0, y_ref[here] + 0.9 * (rhs[here] - image))
        y_out[here] = y
        y_half[here] = y.astype(y_half.dtype)


def whole_dual_kernel(y_ref, rhs, image, y_out, y_half):
    y = jnp.maximum(0.0, y_ref[...] + 0.9 * (rhs[...] - image[...]))
    y_out[...] = y
    y_half[...] = y.astype(y_half.dtype)


def to_blocks(a):
    return jnp.transpose(a.reshape(a.shape[0], -1, BS), (1, 0, 2))


def from_blocks(a):
    return jnp.transpose(a, (1, 0, 2)).reshape(a.shape[1], -1)


def per_device(
    cost, rhs, primal, dual, bound_kind, upper, kblocks, block_row, block_col, block_count
):
    n_col, n_row = lax.axis_size("col"), lax.axis_size("row")
    scen = primal.shape[0]
    span, cols = dual.shape[2] // BS, primal.shape[2] // BS
    row_blocks, col_blocks = span * n_col, cols * n_row
    direct = n_col in (4, 8) and span & (span - 1) == 0
    half = n_col // 2

    tile = kblocks[0, 0]
    slots = jnp.arange(tile.shape[0], dtype=jnp.int32)
    count = block_count[0, 0]
    live = slots < count
    groups = ((count + UNROLL - 1) // UNROLL).reshape(1)
    mine = block_col[0, 0] // cols == lax.axis_index("row")
    bcol = jnp.where(mine, 0, cols) + block_col[0, 0] % cols
    brow = block_row[0, 0]
    if direct:
        brow = brow ^ (lax.axis_index("col") * span)
    to_col = jnp.where(live, bcol, col_blocks)
    to_row = jnp.where(live, brow, row_blocks)

    def swap(a):
        return lax.ppermute(a, "row", [(i, n_row - 1 - i) for i in range(n_row)])

    def partner(a, m):
        return lax.ppermute(a, "col", [(i, i ^ m) for i in range(n_col)])

    def near(a):
        return [partner(a, m) for m in range(1, half)]

    y = to_blocks(dual[:, 0])
    y_half = y.astype(jnp.bfloat16)
    rhs_all = to_blocks(rhs[:, 0])
    if direct:
        y_half = jnp.concatenate([y_half, partner(y_half, half)])
        pair = jnp.stack([y, rhs_all])
        both = jnp.concatenate([pair, partner(pair, half)], axis=1)
        y, rhs_all = both[0], both[1]

    own = jnp.concatenate(
        [to_blocks(primal[:, 0]), to_blocks(cost[:, 0]), to_blocks(upper), to_blocks(bound_kind).astype(jnp.float32)],
        axis=1,
    )
    state = jnp.concatenate([own, swap(own)])
    x, cost_all = state[:, :scen], state[:, scen : 2 * scen]
    upper_all, kind_all = state[:, 2 * scen : 2 * scen + 1], state[:, 2 * scen + 1 :]

    def shape(blocks, dtype):
        return jax.ShapeDtypeStruct((blocks, scen, BS), dtype)

    def call(kernel, outs, ins, scratch=(), scalars=0):
        return pl.pallas_call(
            kernel,
            out_shape=outs,
            in_specs=[SMEM] * scalars + [VMEM] * ins,
            out_specs=tuple(VMEM for _ in outs),
            scratch_shapes=[pltpu.VMEM((blocks, scen, BS), dtype) for blocks, dtype in scratch],
            compiler_params=PARAMS,
            name=kernel.__name__,
        )

    f32, bf16 = jnp.float32, jnp.bfloat16
    backward = call(
        backward_kernel if direct else whole_backward_kernel,
        (shape(col_blocks, f32),),
        1 + (half if direct else 1),
        ((row_blocks, bf16), (col_blocks + 1, f32)) if direct else ((col_blocks + 1, f32),),
        3,
    )
    if direct:
        pieces = (shape(2 * span, f32),) + (shape(2 * span, bf16),) * (half - 1)
    else:
        pieces = (shape(row_blocks, f32),)
    forward = call(
        forward_kernel,
        (shape(col_blocks, f32),) + pieces,
        7,
        ((col_blocks, bf16), (row_blocks + 1, f32)),
        3,
    )

    for step in range(ITERS):
        last = step == ITERS - 1
        y_slab = [y_half] + near(y_half) if direct else [lax.all_gather(y_half, "col", axis=0, tiled=True)]
        (grad,) = backward(groups, brow, to_col, tile, *y_slab)
        x, *image = forward(groups, bcol, to_row, tile, grad, swap(grad), x, cost_all, kind_all, upper_all)
        if direct:
            image = image[:1] + [partner(image[m], m) for m in range(1, half)]
            kept = 1 if last else 2
            total, sent = call(near_sum_kernel, (shape(2 * span, f32), shape(kept * span, bf16)), half)(*image)
            y, y_half = call(dual_kernel, (shape(kept * span, f32), shape(kept * span, bf16)), 4)(
                y, rhs_all, total, partner(sent, half)
            )
        else:
            image = lax.psum_scatter(image[0], "col", scatter_dimension=0, tiled=True)
            y, y_half = call(whole_dual_kernel, (shape(span, f32), shape(span, bf16)), 3)(y, rhs_all, image)

    return (from_blocks(x[:cols])[:, None, :], from_blocks(y)[:, None, :])


def solution(mesh):
    return jax.shard_map(
        per_device,
        mesh=mesh,
        in_specs=(
            P("grp", "col", "row"),
            P("grp", "row", "col"),
            P("grp", "col", "row"),
            P("grp", "row", "col"),
            P(("grp", "col"), "row"),
            P(("grp", "col"), "row"),
            P(("grp", "col"), "row", None, None, None),
            P(("grp", "col"), "row", None),
            P(("grp", "col"), "row", None),
            P(("grp", "col"), "row"),
        ),
        out_specs=(P("grp", "col", "row"), P("grp", "row", "col")),
        check_vma=False,
    )
```

```python
import functools

import jax
import jax.numpy as jnp
from jax import lax
from jax.experimental import pallas as pl
from jax.experimental.pallas import tpu as pltpu
from jax.sharding import PartitionSpec as P

BS = 128
ITERS = 6
WIDE, NARROW = 32, 8
NN = (((1,), (0,)), ((), ()))
NT = (((1,), (1,)), ((), ()))

SMEM = pl.BlockSpec(memory_space=pltpu.SMEM)
VMEM = pl.BlockSpec(memory_space=pltpu.VMEM)
PARAMS = pltpu.CompilerParams(vmem_limit_bytes=24 * 2**20)


class Plan:
    def __init__(self, ref, slots, columns):
        self.ref = ref
        self.pairs = plan_pairs(slots, columns)

    def slot(self, i):
        return 8 + i

    def row(self, i):
        return 8 + 2 * self.pairs + i

    def col(self, pair):
        return 8 + 4 * self.pairs + pair


def plan_pairs(slots, columns):
    return -(-(slots + columns) // (2 * NARROW)) * NARROW


def prepare_kernel(columns, rows, place, brow, bcol, blocks, plan_ref, tile, ends, sem):
    copy = pltpu.make_async_copy(blocks, tile, sem)
    copy.start()
    count, row_flip, col_flip = place[0], place[1], place[2]
    plan = Plan(plan_ref, brow.shape[0], columns)

    for c in range(columns + 1):
        ends[c] = 0

    def column(n):
        return jnp.where(n < count, bcol[n] ^ col_flip, columns)

    def tally(n, _):
        c = column(n)
        ends[c] = ends[c] + 1
        return 0

    lax.fori_loop(0, brow.shape[0], tally, 0, unroll=16)

    def fill(at):
        plan_ref[plan.slot(at)] = 0
        plan_ref[plan.row(at)] = rows
        plan_ref[plan.col(at // 2)] = 0

    start = jnp.int32(0)
    for c in range(columns):
        size = ends[c]
        ends[c] = start
        fill(start + size)
        start = start + ((size + 1) // 2) * 2
    size = ends[columns]
    ends[columns] = start
    plan_ref[0] = start // 2
    for i in range(columns):
        fill(jnp.minimum(start + size + i, 2 * plan.pairs - 1))

    def put(n, _):
        c = column(n)
        at = ends[c]
        ends[c] = at + 1
        plan_ref[plan.slot(at)] = n
        plan_ref[plan.row(at)] = jnp.where(n < count, brow[n] ^ row_flip, rows)
        plan_ref[plan.col(at // 2)] = jnp.where(n < count, c, 0)
        return 0

    lax.fori_loop(0, brow.shape[0], put, 0, unroll=16)
    copy.wait()


def over_pairs(pairs, step):
    wide = pairs // WIDE

    def run(i, _, size, start):
        step(start + i * size, size)
        return 0

    lax.fori_loop(0, wide, functools.partial(run, size=WIDE, start=0), 0)
    rest = wide * WIDE
    lax.fori_loop(0, (pairs - rest + NARROW - 1) // NARROW, functools.partial(run, size=NARROW, start=rest), 0)


def transposed_products(plan_ref, tile, vecs, acc):
    plan = Plan(plan_ref, tile.shape[0], acc.shape[0])

    def step(first, n):
        terms = []
        for u in range(n):
            i = 2 * (first + u)
            left = [vecs[plan_ref[plan.row(i + k)]] for k in range(2)]
            right = [tile[plan_ref[plan.slot(i + k)]] for k in range(2)]
            terms.append(
                lax.dot_general(
                    jnp.concatenate(left, axis=1), jnp.concatenate(right, axis=0), NN, preferred_element_type=jnp.float32
                )
            )
        for u in range(n):
            acc[plan_ref[plan.col(first + u)]] += terms[u]

    acc[...] = jnp.zeros(acc.shape, acc.dtype)
    over_pairs(plan_ref[0], step)


def products(plan_ref, tile, vecs, acc):
    plan = Plan(plan_ref, tile.shape[0], vecs.shape[0])

    def step(first, n):
        terms = []
        for u in range(n):
            i = 2 * (first + u)
            right = [tile[plan_ref[plan.slot(i + k)]] for k in range(2)]
            terms.append(
                lax.dot_general(
                    vecs[plan_ref[plan.col(first + u)]],
                    jnp.concatenate(right, axis=0),
                    NT,
                    preferred_element_type=jnp.float32,
                )
            )
        for u in range(n):
            for k in range(2):
                acc[plan_ref[plan.row(2 * (first + u) + k)]] += terms[u][:, k * BS : (k + 1) * BS]

    acc[...] = jnp.zeros(acc.shape, acc.dtype)
    over_pairs(plan_ref[0], step)


def backward_kernel(plan, tile, *refs):
    pieces, (grad, vecs) = refs[:-2], refs[-2:]
    half = len(pieces)
    span = pieces[0].shape[0] // 2
    for m in range(half):
        vecs[pl.ds(m * span, span)] = pieces[m][pl.ds(0, span)]
        vecs[pl.ds((m + half) * span, span)] = pieces[m][pl.ds(span, span)]
    vecs[2 * half * span] = jnp.zeros(vecs.shape[1:], vecs.dtype)
    transposed_products(plan, tile, vecs, grad)


def forward_kernel(plan, tile, own, other, x_ref, cost, kind, upper, *refs):
    x_out, pieces, (vecs, acc) = refs[0], refs[1:-2], refs[-2:]
    cols = x_ref.shape[0] // 2
    for h in range(2):
        here, there = pl.ds(h * cols, cols), pl.ds((1 - h) * cols, cols)
        x = x_ref[here]
        value = x - 0.4 * (cost[here] - (own[here] + other[there]))
        lifted = jnp.where(kind[here] == 2, value, jnp.maximum(value, 0.0))
        x_next = jnp.where(kind[here] == 1, jnp.minimum(lifted, upper[here]), lifted)
        x_out[here] = x_next
        vecs[here] = (2.0 * x_next - x).astype(vecs.dtype)
    products(plan, tile, vecs, acc)
    half = len(pieces)
    span = pieces[0].shape[0] // 2
    for m in range(half):
        pieces[m][pl.ds(0, span)] = acc[pl.ds(m * span, span)].astype(pieces[m].dtype)
        pieces[m][pl.ds(span, span)] = acc[pl.ds((m + half) * span, span)].astype(pieces[m].dtype)


def near_sum_kernel(own, *refs):
    pieces, (total, sent) = refs[:-2], refs[-2:]
    image = own[...]
    for piece in pieces:
        image = image + piece[...].astype(jnp.float32)
    total[...] = image
    n = sent.shape[0]
    sent[...] = image[image.shape[0] - n :].astype(sent.dtype)


def dual_kernel(y_ref, rhs, near, far, y_out, y_half):
    span = near.shape[0] // 2
    for h in range(y_out.shape[0] // span):
        here = pl.ds(h * span, span)
        there = pl.ds(far.shape[0] - (h + 1) * span, span)
        image = near[here] + far[there].astype(jnp.float32)
        y = jnp.maximum(0.0, y_ref[here] + 0.9 * (rhs[here] - image))
        y_out[here] = y
        y_half[here] = y.astype(y_half.dtype)


def whole_dual_kernel(y_ref, rhs, image, y_out, y_half):
    y = jnp.maximum(0.0, y_ref[...] + 0.9 * (rhs[...] - image[...]))
    y_out[...] = y
    y_half[...] = y.astype(y_half.dtype)


def to_blocks(a):
    return jnp.transpose(a.reshape(a.shape[0], -1, BS), (1, 0, 2))


def from_blocks(a):
    return jnp.transpose(a, (1, 0, 2)).reshape(a.shape[1], -1)


def per_device(
    cost, rhs, primal, dual, bound_kind, upper, kblocks, block_row, block_col, block_count
):
    n_col, n_row = lax.axis_size("col"), lax.axis_size("row")
    scen = primal.shape[0]
    span, cols = dual.shape[2] // BS, primal.shape[2] // BS
    row_blocks, col_blocks = span * n_col, cols * n_row
    direct = n_col in (4, 8) and span & (span - 1) == 0
    half = n_col // 2

    blocks = kblocks[0, 0]
    slots = blocks.shape[0]
    row_flip = lax.axis_index("col") * span if direct else 0
    place = jnp.stack([block_count[0, 0], row_flip, lax.axis_index("row") * cols]).astype(jnp.int32)
    plan, tile = pl.pallas_call(
        functools.partial(prepare_kernel, col_blocks, row_blocks),
        out_shape=(
            jax.ShapeDtypeStruct((8 + 5 * plan_pairs(slots, col_blocks),), jnp.int32),
            pltpu.VMEM(blocks.shape, blocks.dtype),
        ),
        in_specs=[SMEM] * 3 + [pl.BlockSpec(memory_space=pltpu.HBM)],
        out_specs=(SMEM, VMEM),
        scratch_shapes=[pltpu.SMEM((col_blocks + 1,), jnp.int32), pltpu.SemaphoreType.DMA],
        compiler_params=PARAMS,
        name="prepare_kernel",
    )(place, block_row[0, 0], block_col[0, 0], pltpu.with_memory_space_constraint(blocks, pltpu.HBM))

    def swap(a):
        return lax.ppermute(a, "row", [(i, n_row - 1 - i) for i in range(n_row)])

    def partner(a, m):
        return lax.ppermute(a, "col", [(i, i ^ m) for i in range(n_col)])

    def near(a):
        return [partner(a, m) for m in range(1, half)]

    y = to_blocks(dual[:, 0])
    y_half = y.astype(jnp.bfloat16)
    rhs_all = to_blocks(rhs[:, 0])
    if direct:
        y_half = jnp.concatenate([y_half, partner(y_half, half)])

    own = jnp.concatenate(
        [to_blocks(primal[:, 0]), to_blocks(cost[:, 0]), to_blocks(upper), to_blocks(bound_kind).astype(jnp.float32)],
        axis=1,
    )
    state = jnp.concatenate([own, swap(own)])
    x, cost_all = state[:, :scen], state[:, scen : 2 * scen]
    upper_all, kind_all = state[:, 2 * scen : 2 * scen + 1], state[:, 2 * scen + 1 :]

    def shape(blocks, dtype):
        return jax.ShapeDtypeStruct((blocks, scen, BS), dtype)

    def call(kernel, outs, ins, scratch=(), scalars=0):
        return pl.pallas_call(
            kernel,
            out_shape=outs,
            in_specs=[SMEM] * scalars + [VMEM] * ins,
            out_specs=tuple(VMEM for _ in outs),
            scratch_shapes=[pltpu.VMEM((blocks, scen, BS), dtype) for blocks, dtype in scratch],
            compiler_params=PARAMS,
            name=kernel.__name__,
        )

    f32, bf16 = jnp.float32, jnp.bfloat16
    if direct:
        backward = call(backward_kernel, (shape(col_blocks, f32),), 1 + half, ((row_blocks + 1, bf16),), 1)
        pieces = (shape(2 * span, f32),) + (shape(2 * span, bf16),) * (half - 1)
    else:
        backward = call(backward_kernel, (shape(col_blocks, f32),), 2, ((row_blocks + 1, bf16),), 1)
        pieces = (shape(row_blocks, f32),)
    forward = call(
        forward_kernel, (shape(col_blocks, f32),) + pieces, 7, ((col_blocks, bf16), (row_blocks + 1, f32)), 1
    )

    for step in range(ITERS):
        last = step == ITERS - 1
        y_slab = [y_half] + near(y_half) if direct else [lax.all_gather(y_half, "col", axis=0, tiled=True)]
        if direct and step == 0:
            pair, *y_slab = lax.optimization_barrier([jnp.stack([y, rhs_all])] + y_slab)
            both = jnp.concatenate([pair, partner(pair, half)], axis=1)
            y, rhs_all = both[0], both[1]
        (grad,) = backward(plan, tile, *y_slab)
        x, *image = forward(plan, tile, grad, swap(grad), x, cost_all, kind_all, upper_all)
        if direct:
            image = image[:1] + [partner(image[m], m) for m in range(1, half)]
            kept = 1 if last else 2
            total, sent = call(near_sum_kernel, (shape(2 * span, f32), shape(kept * span, bf16)), half)(*image)
            y, y_half = call(dual_kernel, (shape(kept * span, f32), shape(kept * span, bf16)), 4)(
                y, rhs_all, total, partner(sent, half)
            )
        else:
            image = lax.psum_scatter(image[0], "col", scatter_dimension=0, tiled=True)
            y, y_half = call(whole_dual_kernel, (shape(span, f32), shape(span, bf16)), 3)(y, rhs_all, image)

    return (from_blocks(x[:cols])[:, None, :], from_blocks(y)[:, None, :])


def solution(mesh):
    return jax.shard_map(
        per_device,
        mesh=mesh,
        in_specs=(
            P("grp", "col", "row"),
            P("grp", "row", "col"),
            P("grp", "col", "row"),
            P("grp", "row", "col"),
            P(("grp", "col"), "row"),
            P(("grp", "col"), "row"),
            P(("grp", "col"), "row", None, None, None),
            P(("grp", "col"), "row", None),
            P(("grp", "col"), "row", None),
            P(("grp", "col"), "row"),
        ),
        out_specs=(P("grp", "col", "row"), P("grp", "row", "col")),
        check_vma=False,
    )
```

```python
import functools

import jax
import jax.numpy as jnp
from jax import lax
from jax.experimental import pallas as pl
from jax.experimental.pallas import tpu as pltpu
from jax.sharding import PartitionSpec as P

BS = 128
ITERS = 6
WIDE, NARROW = 48, 16
NN = (((1,), (0,)), ((), ()))
NT = (((1,), (1,)), ((), ()))

SMEM = pl.BlockSpec(memory_space=pltpu.SMEM)
VMEM = pl.BlockSpec(memory_space=pltpu.VMEM)
HBM = pl.BlockSpec(memory_space=pltpu.HBM)
PARAMS = pltpu.CompilerParams(vmem_limit_bytes=24 * 2**20)


class Plan:
    def __init__(self, ref, slots, columns):
        self.ref = ref
        self.pairs, self.room = plan_size(slots, columns)

    def first(self, near):
        return self.ref[0] if near else 0

    def count(self, near):
        return self.ref[2] if near else self.ref[1]

    def slot(self, i):
        return 8 + i

    def row(self, i):
        return 8 + 2 * self.room + i

    def col(self, pair):
        return 8 + 4 * self.room + pair


def plan_size(slots, columns):
    pairs = -(-(slots + 2 * columns) // (2 * NARROW)) * NARROW + 2 * NARROW
    return pairs, pairs + -(-slots // 2)


def setup_kernel(direct, half, count, *refs):
    given, (state, duals, y_half, order), held, sems = refs[:8], refs[8:12], refs[12:20], refs[20]
    copies = [pltpu.make_async_copy(a, b, sems.at[i]) for i, (a, b) in enumerate(zip(given, held))]
    for copy in copies:
        copy.start()
    for copy in copies:
        copy.wait()
    primal, cost, upper, kind, dual, rhs, brow, bcol = held
    cols, span, scen = state.shape[0], dual.shape[1], dual.shape[0]
    for b in range(cols):
        state[b, pl.ds(0, scen)] = primal[:, b, :]
        state[b, pl.ds(scen, scen)] = cost[:, b, :]
        state[b, pl.ds(2 * scen, 1)] = upper[pl.ds(b, 1)]
        state[b, pl.ds(2 * scen + 1, 1)] = kind[pl.ds(b, 1)].astype(jnp.float32)
    for b in range(span):
        y = dual[:, b, :]
        duals[b] = y
        duals[span + b] = rhs[:, b, :]
        y_half[b] = y.astype(y_half.dtype)
    columns = 2 * cols
    key = bcol[...] ^ (lax.axis_index("row") * cols)
    row = brow[...]
    if direct:
        row = row ^ (lax.axis_index("col") * span)
        key = key + jnp.where((row & ((half - 1) * span)) == 0, 0, columns)
    lanes = key.shape[1]
    slot = lanes * lax.broadcasted_iota(jnp.int32, key.shape, 0) + lax.broadcasted_iota(jnp.int32, key.shape, 1)
    order[pl.ds(0, key.shape[0])] = jnp.where(slot < count[0, 0], key, 2 * columns)
    order[pl.ds(key.shape[0], key.shape[0])] = row


def runs_of(count, step, run=16):
    def body(i, _):
        for k in range(run):
            step(i * run + k)
        return 0

    lax.fori_loop(0, count // run, body, 0)


def prepare_kernel(columns, rows, order, blocks, plan_ref, tile, keys, ends, sem, key_sems):
    copy = pltpu.make_async_copy(blocks, tile, sem)
    copy.start()
    key_copies = [
        pltpu.make_async_copy(order.at[i], keys.at[pl.ds(i * BS, BS)], key_sems.at[i]) for i in range(order.shape[0])
    ]
    for key_copy in key_copies:
        key_copy.start()
    slots = blocks.shape[0]
    plan = Plan(plan_ref, slots, columns)

    def clear(i, _):
        for k in range(2):
            plan_ref[plan.slot(2 * i + k)] = 0
            plan_ref[plan.row(2 * i + k)] = rows
        plan_ref[plan.col(i)] = 0
        return 0

    lax.fori_loop(0, plan.pairs, clear, 0, unroll=16)
    for c in range(2 * columns):
        ends[c] = 0
    for key_copy in key_copies:
        key_copy.wait()

    def tally(n):
        key = keys[n]
        ends[key] = ends[key] + 1

    ends[2 * columns] = 0
    runs_of(slots, tally)

    start = jnp.int32(0)
    for near in range(2):
        plan_ref[near] = start // 2
        first = start
        for c in range(near * columns, (near + 1) * columns):
            size = ends[c]
            ends[c] = start
            start = start + ((size + 1) // 2) * 2
        plan_ref[1 + near] = (start - first) // 2
        start = (start + 2 * NARROW - 1) // (2 * NARROW) * (2 * NARROW)
        if near == 0:
            plan_ref[0] = start // 2
    ends[2 * columns] = 2 * plan.pairs

    def put(n):
        key = keys[n]
        at = ends[key]
        ends[key] = at + 1
        plan_ref[plan.slot(at)] = n
        plan_ref[plan.row(at)] = keys[slots + n]
        plan_ref[plan.col(at // 2)] = lax.rem(key, columns)

    runs_of(slots, put)
    copy.wait()


def over_pairs(plan, near, step):
    begin, pairs = plan.first(near), plan.count(near)
    wide = pairs // WIDE

    def run(i, _, size, start):
        step(start + i * size, size)
        return 0

    lax.fori_loop(0, wide, functools.partial(run, size=WIDE, start=begin), 0)
    rest = wide * WIDE
    lax.fori_loop(0, (pairs - rest + NARROW - 1) // NARROW, functools.partial(run, size=NARROW, start=begin + rest), 0)


def transposed_products(plan, near, tile, vecs, acc):
    ref = plan.ref

    def step(first, n):
        terms = []
        for u in range(n):
            i = 2 * (first + u)
            left = [vecs[ref[plan.row(i + k)]] for k in range(2)]
            right = [tile[ref[plan.slot(i + k)]] for k in range(2)]
            terms.append(
                lax.dot_general(
                    jnp.concatenate(left, axis=1), jnp.concatenate(right, axis=0), NN, preferred_element_type=jnp.float32
                )
            )
        for u in range(n):
            acc[ref[plan.col(first + u)]] += terms[u]

    over_pairs(plan, near, step)


def products(plan, near, tile, vecs, acc):
    ref = plan.ref

    def step(first, n):
        terms = []
        for u in range(n):
            i = 2 * (first + u)
            right = [tile[ref[plan.slot(i + k)]] for k in range(2)]
            terms.append(
                lax.dot_general(
                    vecs[ref[plan.col(first + u)]], jnp.concatenate(right, axis=0), NT, preferred_element_type=jnp.float32
                )
            )
        for u in range(n):
            for k in range(2):
                acc[ref[plan.row(2 * (first + u) + k)]] += terms[u][:, k * BS : (k + 1) * BS]

    acc[...] = jnp.zeros(acc.shape, acc.dtype)
    over_pairs(plan, near, step)


def backward_own_kernel(plan_ref, tile, piece, grad, vecs):
    plan = Plan(plan_ref, tile.shape[0], grad.shape[0])
    span = piece.shape[0] // 2
    rows = vecs.shape[0] - 1
    vecs[pl.ds(0, span)] = piece[pl.ds(0, span)]
    vecs[pl.ds(rows // 2, span)] = piece[pl.ds(span, span)]
    vecs[rows] = jnp.zeros(vecs.shape[1:], vecs.dtype)
    grad[...] = jnp.zeros(grad.shape, grad.dtype)
    transposed_products(plan, False, tile, vecs, grad)


def backward_near_kernel(plan_ref, tile, *refs):
    pieces, (begun, grad, vecs) = refs[:-3], refs[-3:]
    plan = Plan(plan_ref, tile.shape[0], grad.shape[0])
    half = len(pieces) + 1
    span = pieces[0].shape[0] // 2
    for m in range(1, half):
        vecs[pl.ds(m * span, span)] = pieces[m - 1][pl.ds(0, span)]
        vecs[pl.ds((m + half) * span, span)] = pieces[m - 1][pl.ds(span, span)]
    vecs[2 * half * span] = jnp.zeros(vecs.shape[1:], vecs.dtype)
    grad[...] = begun[...]
    transposed_products(plan, True, tile, vecs, grad)


def primal_step(own, other, here_state, there_state, x_ref, x_out, x_bar):
    cols, scen = here_state.shape[0], own.shape[1]
    for h, state in enumerate((here_state, there_state)):
        here, there = pl.ds(h * cols, cols), pl.ds((1 - h) * cols, cols)
        x = state[:, pl.ds(0, scen)] if x_ref is None else x_ref[here]
        cost = state[:, pl.ds(scen, scen)]
        upper, kind = state[:, pl.ds(2 * scen, 1)], state[:, pl.ds(2 * scen + 1, 1)]
        value = x - 0.4 * (cost - (own[here] + other[there]))
        lifted = jnp.where(kind == 2, value, jnp.maximum(value, 0.0))
        x_next = jnp.where(kind == 1, jnp.minimum(lifted, upper), lifted)
        if x_out.shape[0] == 2 * cols:
            x_out[here] = x_next
        elif h == 0:
            for b in range(cols):
                x_out[:, b, :] = x_next[b]
        x_bar[here] = (2.0 * x_next - x).astype(x_bar.dtype)


def forward_near_kernel(first, plan_ref, tile, own, other, here_state, there_state, *refs):
    x_ref = None if first else refs[0]
    x_out, x_bar, *pieces, acc = refs if first else refs[1:]
    primal_step(own, other, here_state, there_state, x_ref, x_out, x_bar)
    if pieces:
        products(Plan(plan_ref, tile.shape[0], x_bar.shape[0]), True, tile, x_bar, acc)
        half = len(pieces) + 1
        span = pieces[0].shape[0] // 2
        for m in range(1, half):
            pieces[m - 1][pl.ds(0, span)] = acc[pl.ds(m * span, span)].astype(pieces[m - 1].dtype)
            pieces[m - 1][pl.ds(span, span)] = acc[pl.ds((m + half) * span, span)].astype(pieces[m - 1].dtype)


def forward_own_kernel(plan_ref, tile, x_bar, piece, acc):
    products(Plan(plan_ref, tile.shape[0], x_bar.shape[0]), False, tile, x_bar, acc)
    span = piece.shape[0] // 2
    piece[pl.ds(0, span)] = acc[pl.ds(0, span)]
    piece[pl.ds(span, span)] = acc[pl.ds((acc.shape[0] - 1) // 2, span)]


def near_sum_kernel(duals, own, *refs):
    pieces, (total, sent) = refs[:-2], refs[-2:]
    image = own[...]
    for piece in pieces:
        image = image + piece[...].astype(jnp.float32)
    total[...] = image
    span = image.shape[0] // 2
    at = sent.shape[0] - span
    sent[pl.ds(at, span)] = image[span:].astype(sent.dtype)
    if at:
        sent[pl.ds(0, span)] = (image[:span] - duals[pl.ds(span, span)]).astype(sent.dtype)


def dual_kernel(duals, near, far, y_own, y_far, y_out, y_half):
    span = near.shape[0] // 2
    here, there = pl.ds(0, span), pl.ds(span, span)
    own = y_own[here] + 0.9 * (duals[there] - (near[here] + far[there].astype(jnp.float32)))
    copy = y_far[there].astype(jnp.float32) - 0.9 * (far[here].astype(jnp.float32) + near[there])
    for at, y in ((here, jnp.maximum(0.0, own)), (there, jnp.maximum(0.0, copy))):
        y_out[at] = y
        y_half[at] = y.astype(y_half.dtype)


def last_dual_kernel(duals, near, far, y_own, y_out):
    span = far.shape[0]
    here, there = pl.ds(0, span), pl.ds(span, span)
    own = y_own[here] + 0.9 * (duals[there] - (near[here] + far[...].astype(jnp.float32)))
    y = jnp.maximum(0.0, own)
    for b in range(span):
        y_out[:, b, :] = y[b]


def whole_dual_kernel(y_ref, rhs, image, y_out, y_half):
    y = jnp.maximum(0.0, y_ref[...] + 0.9 * (rhs[...] - image[...]))
    y_out[...] = y
    y_half[...] = y.astype(y_half.dtype)


def in_blocks(a):
    return a.reshape(tuple(n for n in a.shape[:-1] if n > 1) + (-1, BS))


def per_device(
    cost, rhs, primal, dual, bound_kind, upper, kblocks, block_row, block_col, block_count
):
    n_col, n_row = lax.axis_size("col"), lax.axis_size("row")
    scen = primal.shape[0]
    span, cols = dual.shape[2] // BS, primal.shape[2] // BS
    row_blocks, col_blocks = span * n_col, cols * n_row
    direct = n_col in (4, 8) and span & (span - 1) == 0
    half = n_col // 2

    f32, bf16, i32 = jnp.float32, jnp.bfloat16, jnp.int32
    blocks = kblocks[0, 0]
    slots = blocks.shape[0]

    def swap(a):
        return lax.ppermute(a, "row", [(i, n_row - 1 - i) for i in range(n_row)])

    def partner(a, m):
        return lax.ppermute(a, "col", [(i, i ^ m) for i in range(n_col)])

    def near(a):
        return [partner(a, m) for m in range(1, half)]

    def shape(blocks, dtype):
        return jax.ShapeDtypeStruct((blocks, scen, BS), dtype)

    def call(kernel, outs, ins, scratch=(), scalars=0, flops=0):
        return pl.pallas_call(
            kernel,
            out_shape=outs,
            in_specs=[SMEM] * scalars + [VMEM] * ins,
            out_specs=tuple(VMEM for _ in outs),
            scratch_shapes=[pltpu.VMEM((blocks, scen, BS), dtype) for blocks, dtype in scratch],
            compiler_params=PARAMS,
            cost_estimate=pl.CostEstimate(flops=flops, bytes_accessed=0, transcendentals=0),
            name=getattr(kernel, "func", kernel).__name__,
        )

    given = [in_blocks(a) for a in (primal, cost, upper, bound_kind, dual, rhs, block_row, block_col)]
    state, duals, y_half, order = pl.pallas_call(
        functools.partial(setup_kernel, direct, half),
        out_shape=(
            jax.ShapeDtypeStruct((cols, 2 * scen + 2, BS), f32),
            shape(2 * span, f32),
            shape(span, bf16),
            jax.ShapeDtypeStruct((2 * slots // BS, BS), i32),
        ),
        in_specs=[SMEM] + [HBM] * 8,
        out_specs=(VMEM,) * 4,
        scratch_shapes=[pltpu.VMEM(a.shape, a.dtype) for a in given] + [pltpu.SemaphoreType.DMA((8,))],
        compiler_params=PARAMS,
        name="setup_kernel",
    )(block_count, *[pltpu.with_memory_space_constraint(a, pltpu.HBM) for a in given])
    other_state = swap(state)
    if direct:
        y_half, order = lax.optimization_barrier((jnp.concatenate([y_half, partner(y_half, half)]), order))
    plan, tile = pl.pallas_call(
        functools.partial(prepare_kernel, col_blocks, row_blocks),
        out_shape=(
            pltpu.SMEM((8 + 5 * plan_size(slots, col_blocks)[1],), i32),
            pltpu.VMEM(blocks.shape, blocks.dtype),
        ),
        in_specs=[VMEM, HBM],
        out_specs=(SMEM, VMEM),
        scratch_shapes=[
            pltpu.SMEM((order.size,), i32),
            pltpu.SMEM((2 * col_blocks + 1,), i32),
            pltpu.SemaphoreType.DMA,
            pltpu.SemaphoreType.DMA((order.shape[0],)),
        ],
        compiler_params=PARAMS,
        name="prepare_kernel",
    )(order, pltpu.with_memory_space_constraint(blocks, pltpu.HBM))

    flops = 2 * slots * BS * BS * scen
    backward_own = call(backward_own_kernel, (shape(col_blocks, f32),), 2, ((row_blocks + 1, bf16),), 1, flops)
    backward_near = call(
        backward_near_kernel, (shape(col_blocks, f32),), 1 + half, ((row_blocks + 1, bf16),), 1, flops
    )
    near_pieces = (shape(2 * span, bf16),) * (half - 1) if direct else ()
    forward_own = call(
        forward_own_kernel,
        (shape(2 * span if direct else row_blocks, f32),),
        2,
        ((row_blocks + 1, f32),),
        1,
        flops,
    )

    x = ()
    for step in range(ITERS):
        first, last = step == 0, step == ITERS - 1
        if direct:
            y_near = near(y_half)
            (grad,) = backward_own(plan, tile, y_half)
            (grad,) = backward_near(plan, tile, *y_near, grad)
        else:
            (grad,) = backward_own(plan, tile, lax.all_gather(y_half, "col", axis=0, tiled=True))
        x_shape = jax.ShapeDtypeStruct((scen, cols, BS), f32) if last else shape(col_blocks, f32)
        x, x_bar, *image = call(
            functools.partial(forward_near_kernel, first),
            (x_shape, shape(col_blocks, bf16)) + near_pieces,
            5 if first else 6,
            ((row_blocks + 1, f32),),
            1,
            flops,
        )(plan, tile, grad, swap(grad), state, other_state, *x)
        x = (x,)
        (own_image,) = forward_own(plan, tile, x_bar)
        if direct:
            image = [partner(image[m - 1], m) for m in range(1, half)]
            kept = 1 if last else 2
            total, sent = call(near_sum_kernel, (shape(2 * span, f32), shape(kept * span, bf16)), 1 + half)(
                duals, own_image, *image
            )
            args = (duals, total, partner(sent, half))
            if last:
                (y,) = call(last_dual_kernel, (jax.ShapeDtypeStruct((scen, span, BS), f32),), 4)(*args, y)
            else:
                y_own, y_far = (duals, y_half) if first else (y, y)
                y, y_half = call(dual_kernel, (shape(2 * span, f32), shape(2 * span, bf16)), 5)(*args, y_own, y_far)
        else:
            image = lax.psum_scatter(own_image, "col", scatter_dimension=0, tiled=True)
            y, y_half = call(whole_dual_kernel, (shape(span, f32), shape(span, bf16)), 3)(
                duals[:span] if first else y, duals[span:], image
            )

    y = y if direct else jnp.transpose(y, (1, 0, 2))
    return (x[0].reshape(scen, 1, -1), y.reshape(scen, 1, -1))


def solution(mesh):
    return jax.shard_map(
        per_device,
        mesh=mesh,
        in_specs=(
            P("grp", "col", "row"),
            P("grp", "row", "col"),
            P("grp", "col", "row"),
            P("grp", "row", "col"),
            P(("grp", "col"), "row"),
            P(("grp", "col"), "row"),
            P(("grp", "col"), "row", None, None, None),
            P(("grp", "col"), "row", None),
            P(("grp", "col"), "row", None),
            P(("grp", "col"), "row"),
        ),
        out_specs=(P("grp", "col", "row"), P("grp", "row", "col")),
        check_vma=False,
    )
```

```python
import functools

import jax
import jax.numpy as jnp
from jax import lax
from jax.experimental import pallas as pl
from jax.experimental.pallas import tpu as pltpu
from jax.sharding import PartitionSpec as P

BS = 128
ITERS = 6
WIDE, NARROW = (48, 112), 16
NN = (((1,), (0,)), ((), ()))
NT = (((1,), (1,)), ((), ()))

SMEM = pl.BlockSpec(memory_space=pltpu.SMEM)
VMEM = pl.BlockSpec(memory_space=pltpu.VMEM)
HBM = pl.BlockSpec(memory_space=pltpu.HBM)
PARAMS = pltpu.CompilerParams(vmem_limit_bytes=24 * 2**20)


class Plan:
    def __init__(self, ref, slots, columns):
        self.ref = ref
        self.pairs, self.room = plan_size(slots, columns)

    def first(self, near):
        return self.ref[0] if near else 0

    def runs(self, near):
        return self.ref[1 + 2 * near], self.ref[2 + 2 * near]

    def slot(self, i):
        return 8 + i

    def row(self, i):
        return 8 + 2 * self.room + i

    def col(self, pair):
        return 8 + 4 * self.room + pair


def plan_size(slots, columns):
    pairs = -(-(slots + 2 * columns) // (2 * NARROW)) * NARROW + sum(WIDE)
    return pairs, pairs + -(-slots // 2)


def setup_kernel(direct, half, count, *refs):
    given, (state, duals, y_half, order), held, sems = refs[:8], refs[8:12], refs[12:20], refs[20]
    copies = [pltpu.make_async_copy(a, b, sems.at[i]) for i, (a, b) in enumerate(zip(given, held))]
    for copy in copies:
        copy.start()
    for copy in copies:
        copy.wait()
    primal, cost, upper, kind, dual, rhs, brow, bcol = held
    cols, span, scen = state.shape[0], dual.shape[1], dual.shape[0]
    for b in range(cols):
        state[b, pl.ds(0, scen)] = primal[:, b, :]
        state[b, pl.ds(scen, scen)] = cost[:, b, :]
        state[b, pl.ds(2 * scen, 1)] = upper[pl.ds(b, 1)]
        state[b, pl.ds(2 * scen + 1, 1)] = kind[pl.ds(b, 1)].astype(jnp.float32)
    for b in range(span):
        y = dual[:, b, :]
        duals[b] = y
        duals[span + b] = rhs[:, b, :]
        y_half[b] = y.astype(y_half.dtype)
    columns = 2 * cols
    key = bcol[...] ^ (lax.axis_index("row") * cols)
    row = brow[...]
    if direct:
        row = row ^ (lax.axis_index("col") * span)
        key = key + jnp.where((row & ((half - 1) * span)) == 0, 0, columns)
    lanes = key.shape[1]
    slot = lanes * lax.broadcasted_iota(jnp.int32, key.shape, 0) + lax.broadcasted_iota(jnp.int32, key.shape, 1)
    order[pl.ds(0, key.shape[0])] = jnp.where(slot < count[0, 0], key, 2 * columns)
    order[pl.ds(key.shape[0], key.shape[0])] = row


def runs_of(count, step, run=16):
    def body(i, _):
        for k in range(run):
            step(i * run + k)
        return 0

    lax.fori_loop(0, count // run, body, 0)


def prepare_kernel(columns, rows, order, blocks, plan_ref, tile, keys, ends, sem, key_sems):
    copy = pltpu.make_async_copy(blocks, tile, sem)
    copy.start()
    key_copies = [
        pltpu.make_async_copy(order.at[i], keys.at[pl.ds(i * BS, BS)], key_sems.at[i]) for i in range(order.shape[0])
    ]
    for key_copy in key_copies:
        key_copy.start()
    slots = blocks.shape[0]
    plan = Plan(plan_ref, slots, columns)

    def clear(i, _):
        for k in range(2):
            plan_ref[plan.slot(2 * i + k)] = 0
            plan_ref[plan.row(2 * i + k)] = rows
        plan_ref[plan.col(i)] = 0
        return 0

    lax.fori_loop(0, plan.pairs, clear, 0, unroll=16)
    for c in range(2 * columns):
        ends[c] = 0
    for key_copy in key_copies:
        key_copy.wait()

    def tally(n):
        key = keys[n]
        ends[key] = ends[key] + 1

    ends[2 * columns] = 0
    runs_of(slots, tally)

    start = jnp.int32(0)
    for near in range(2):
        first = start
        for c in range(near * columns, (near + 1) * columns):
            size = ends[c]
            ends[c] = start
            start = start + ((size + 1) // 2) * 2
        pairs = (start - first) // 2
        wide = (pairs + WIDE[near] - 1 - 3 * NARROW) // WIDE[near]
        narrow = (jnp.maximum(pairs - wide * WIDE[near], 0) + NARROW - 1) // NARROW
        plan_ref[1 + 2 * near] = wide
        plan_ref[2 + 2 * near] = narrow
        start = first + 2 * (wide * WIDE[near] + narrow * NARROW)
        if near == 0:
            plan_ref[0] = start // 2
    ends[2 * columns] = 2 * plan.pairs

    def put(n):
        key = keys[n]
        at = ends[key]
        ends[key] = at + 1
        plan_ref[plan.slot(at)] = n
        plan_ref[plan.row(at)] = keys[slots + n]
        plan_ref[plan.col(at // 2)] = lax.rem(key, columns)

    runs_of(slots, put)
    copy.wait()


def over_pairs(plan, near, step):
    begin, (wide, narrow) = plan.first(near), plan.runs(near)

    def run(i, _, size, start):
        step(start + i * size, size)
        return 0

    lax.fori_loop(0, wide, functools.partial(run, size=WIDE[near], start=begin), 0)
    begin = begin + wide * WIDE[near]
    lax.fori_loop(0, narrow, functools.partial(run, size=NARROW, start=begin), 0)


def transposed_products(plan, near, tile, vecs, acc):
    ref = plan.ref

    def step(first, n):
        terms = []
        for u in range(n):
            i = 2 * (first + u)
            left = [vecs[ref[plan.row(i + k)]] for k in range(2)]
            right = [tile[ref[plan.slot(i + k)]] for k in range(2)]
            terms.append(
                lax.dot_general(
                    jnp.concatenate(left, axis=1), jnp.concatenate(right, axis=0), NN, preferred_element_type=jnp.float32
                )
            )
        for u in range(n):
            acc[ref[plan.col(first + u)]] += terms[u]

    over_pairs(plan, near, step)


def products(plan, near, tile, flipped, vecs, acc):
    ref = plan.ref
    axis, dims = (1, NN) if flipped else (0, NT)

    def step(first, n):
        terms = []
        for u in range(n):
            i = 2 * (first + u)
            right = [tile[ref[plan.slot(i + k)]] for k in range(2)]
            terms.append(
                lax.dot_general(
                    vecs[ref[plan.col(first + u)]],
                    jnp.concatenate(right, axis=axis),
                    dims,
                    preferred_element_type=jnp.float32,
                )
            )
        for u in range(n):
            for k in range(2):
                acc[ref[plan.row(2 * (first + u) + k)]] += terms[u][:, k * BS : (k + 1) * BS]

    acc[...] = jnp.zeros(acc.shape, acc.dtype)
    over_pairs(plan, near, step)


def backward_own_kernel(plan_ref, tile, piece, grad, vecs):
    plan = Plan(plan_ref, tile.shape[0], grad.shape[0])
    span = piece.shape[0] // 2
    rows = vecs.shape[0] - 1
    vecs[pl.ds(0, span)] = piece[pl.ds(0, span)]
    vecs[pl.ds(rows // 2, span)] = piece[pl.ds(span, span)]
    vecs[rows] = jnp.zeros(vecs.shape[1:], vecs.dtype)
    grad[...] = jnp.zeros(grad.shape, grad.dtype)
    transposed_products(plan, False, tile, vecs, grad)


def backward_near_kernel(plan_ref, tile, *refs):
    pieces, (begun, grad, vecs) = refs[:-3], refs[-3:]
    plan = Plan(plan_ref, tile.shape[0], grad.shape[0])
    half = len(pieces) + 1
    span = pieces[0].shape[0] // 2
    for m in range(1, half):
        vecs[pl.ds(m * span, span)] = pieces[m - 1][pl.ds(0, span)]
        vecs[pl.ds((m + half) * span, span)] = pieces[m - 1][pl.ds(span, span)]
    vecs[2 * half * span] = jnp.zeros(vecs.shape[1:], vecs.dtype)
    grad[...] = begun[...]
    transposed_products(plan, True, tile, vecs, grad)


def primal_step(own, other, here_state, there_state, x_ref, x_out, x_bar):
    cols, scen = here_state.shape[0], own.shape[1]
    for h, state in enumerate((here_state, there_state)):
        here, there = pl.ds(h * cols, cols), pl.ds((1 - h) * cols, cols)
        x = state[:, pl.ds(0, scen)] if x_ref is None else x_ref[here]
        cost = state[:, pl.ds(scen, scen)]
        upper, kind = state[:, pl.ds(2 * scen, 1)], state[:, pl.ds(2 * scen + 1, 1)]
        value = x - 0.4 * (cost - (own[here] + other[there]))
        lifted = jnp.where(kind == 2, value, jnp.maximum(value, 0.0))
        x_next = jnp.where(kind == 1, jnp.minimum(lifted, upper), lifted)
        if x_out.shape[0] == 2 * cols:
            x_out[here] = x_next
        elif h == 0:
            for b in range(cols):
                x_out[:, b, :] = x_next[b]
        x_bar[here] = (2.0 * x_next - x).astype(x_bar.dtype)


def forward_near_kernel(first, plan_ref, tile, own, other, here_state, there_state, *refs):
    x_ref = None if first else refs[0]
    x_out, x_bar, *pieces, acc = refs if first else refs[1:]
    primal_step(own, other, here_state, there_state, x_ref, x_out, x_bar)
    if pieces:
        products(Plan(plan_ref, tile.shape[0], x_bar.shape[0]), True, tile, not first, x_bar, acc)
        half = len(pieces) + 1
        span = pieces[0].shape[0] // 2
        for m in range(1, half):
            pieces[m - 1][pl.ds(0, span)] = acc[pl.ds(m * span, span)].astype(pieces[m - 1].dtype)
            pieces[m - 1][pl.ds(span, span)] = acc[pl.ds((m + half) * span, span)].astype(pieces[m - 1].dtype)


def forward_own_kernel(flipped, plan_ref, tile, x_bar, piece, acc):
    products(Plan(plan_ref, tile.shape[0], x_bar.shape[0]), False, tile, flipped, x_bar, acc)
    span = piece.shape[0] // 2
    piece[pl.ds(0, span)] = acc[pl.ds(0, span)]
    piece[pl.ds(span, span)] = acc[pl.ds((acc.shape[0] - 1) // 2, span)]


def flip_kernel(after, tile, flipped, done):
    def run(i, _):
        for k in range(8):
            flipped[i * 8 + k] = tile[i * 8 + k].T
        return 0

    lax.fori_loop(0, tile.shape[0] // 8, run, 0)
    done[...] = jnp.zeros(done.shape, done.dtype)


def near_sum_kernel(duals, own, *refs):
    pieces, (total, sent) = refs[:-2], refs[-2:]
    image = own[...]
    for piece in pieces:
        image = image + piece[...].astype(jnp.float32)
    total[...] = image
    span = image.shape[0] // 2
    at = sent.shape[0] - span
    sent[pl.ds(at, span)] = image[span:].astype(sent.dtype)
    if at:
        sent[pl.ds(0, span)] = (image[:span] - duals[pl.ds(span, span)]).astype(sent.dtype)


def dual_kernel(duals, near, far, y_own, y_far, *refs):
    y_out, y_half = refs[-2:]
    span = near.shape[0] // 2
    here, there = pl.ds(0, span), pl.ds(span, span)
    own = y_own[here] + 0.9 * (duals[there] - (near[here] + far[there].astype(jnp.float32)))
    copy = y_far[there].astype(jnp.float32) - 0.9 * (far[here].astype(jnp.float32) + near[there])
    for at, y in ((here, jnp.maximum(0.0, own)), (there, jnp.maximum(0.0, copy))):
        y_out[at] = y
        y_half[at] = y.astype(y_half.dtype)


def last_dual_kernel(duals, near, far, y_own, y_out):
    span = far.shape[0]
    here, there = pl.ds(0, span), pl.ds(span, span)
    own = y_own[here] + 0.9 * (duals[there] - (near[here] + far[...].astype(jnp.float32)))
    y = jnp.maximum(0.0, own)
    for b in range(span):
        y_out[:, b, :] = y[b]


def whole_dual_kernel(y_ref, rhs, image, y_out, y_half):
    y = jnp.maximum(0.0, y_ref[...] + 0.9 * (rhs[...] - image[...]))
    y_out[...] = y
    y_half[...] = y.astype(y_half.dtype)


def in_blocks(a):
    return a.reshape(tuple(n for n in a.shape[:-1] if n > 1) + (-1, BS))


def per_device(
    cost, rhs, primal, dual, bound_kind, upper, kblocks, block_row, block_col, block_count
):
    n_col, n_row = lax.axis_size("col"), lax.axis_size("row")
    scen = primal.shape[0]
    span, cols = dual.shape[2] // BS, primal.shape[2] // BS
    row_blocks, col_blocks = span * n_col, cols * n_row
    direct = n_col in (4, 8) and span & (span - 1) == 0
    half = n_col // 2

    f32, bf16, i32 = jnp.float32, jnp.bfloat16, jnp.int32
    blocks = kblocks[0, 0]
    slots = blocks.shape[0]

    def swap(a):
        return lax.ppermute(a, "row", [(i, n_row - 1 - i) for i in range(n_row)])

    def partner(a, m):
        return lax.ppermute(a, "col", [(i, i ^ m) for i in range(n_col)])

    def near(a):
        return [partner(a, m) for m in range(1, half)]

    def shape(blocks, dtype):
        return jax.ShapeDtypeStruct((blocks, scen, BS), dtype)

    def call(kernel, outs, ins, scratch=(), scalars=0, flops=0):
        return pl.pallas_call(
            kernel,
            out_shape=outs,
            in_specs=[SMEM] * scalars + [VMEM] * ins,
            out_specs=tuple(VMEM for _ in outs),
            scratch_shapes=[pltpu.VMEM((blocks, scen, BS), dtype) for blocks, dtype in scratch],
            compiler_params=PARAMS,
            cost_estimate=pl.CostEstimate(flops=flops, bytes_accessed=0, transcendentals=0),
            name=getattr(kernel, "func", kernel).__name__,
        )

    given = [in_blocks(a) for a in (primal, cost, upper, bound_kind, dual, rhs, block_row, block_col)]
    state, duals, y_half, order = pl.pallas_call(
        functools.partial(setup_kernel, direct, half),
        out_shape=(
            jax.ShapeDtypeStruct((cols, 2 * scen + 2, BS), f32),
            shape(2 * span, f32),
            shape(span, bf16),
            jax.ShapeDtypeStruct((2 * slots // BS, BS), i32),
        ),
        in_specs=[SMEM] + [HBM] * 8,
        out_specs=(VMEM,) * 4,
        scratch_shapes=[pltpu.VMEM(a.shape, a.dtype) for a in given] + [pltpu.SemaphoreType.DMA((8,))],
        compiler_params=PARAMS,
        name="setup_kernel",
    )(block_count, *[pltpu.with_memory_space_constraint(a, pltpu.HBM) for a in given])
    other_state = swap(state)
    if direct:
        y_half, order = lax.optimization_barrier((jnp.concatenate([y_half, partner(y_half, half)]), order))
    plan, tile = pl.pallas_call(
        functools.partial(prepare_kernel, col_blocks, row_blocks),
        out_shape=(
            pltpu.SMEM((8 + 5 * plan_size(slots, col_blocks)[1],), i32),
            pltpu.VMEM(blocks.shape, blocks.dtype),
        ),
        in_specs=[VMEM, HBM],
        out_specs=(SMEM, VMEM),
        scratch_shapes=[
            pltpu.SMEM((order.size,), i32),
            pltpu.SMEM((2 * col_blocks + 1,), i32),
            pltpu.SemaphoreType.DMA,
            pltpu.SemaphoreType.DMA((order.shape[0],)),
        ],
        compiler_params=PARAMS,
        name="prepare_kernel",
    )(order, pltpu.with_memory_space_constraint(blocks, pltpu.HBM))

    flops = 2 * slots * BS * BS * scen
    backward_own = call(backward_own_kernel, (shape(col_blocks, f32),), 2, ((row_blocks + 1, bf16),), 1, flops)
    backward_near = call(
        backward_near_kernel, (shape(col_blocks, f32),), 1 + half, ((row_blocks + 1, bf16),), 1, flops
    )
    near_pieces = (shape(2 * span, bf16),) * (half - 1) if direct else ()
    x = ()
    for step in range(ITERS):
        first, last = step == 0, step == ITERS - 1
        if direct:
            y_near = near(y_half)
            (grad,) = backward_own(plan, tile, y_half)
            (grad,) = backward_near(plan, tile, *y_near, grad)
        else:
            (grad,) = backward_own(plan, tile, lax.all_gather(y_half, "col", axis=0, tiled=True))
        x_shape = jax.ShapeDtypeStruct((scen, cols, BS), f32) if last else shape(col_blocks, f32)
        x, x_bar, *image = call(
            functools.partial(forward_near_kernel, first),
            (x_shape, shape(col_blocks, bf16)) + near_pieces,
            5 if first else 6,
            ((row_blocks + 1, f32),),
            1,
            flops,
        )(plan, tile if first else flipped, grad, swap(grad), state, other_state, *x)
        x = (x,)
        (own_image,) = call(
            functools.partial(forward_own_kernel, not first),
            (shape(2 * span if direct else row_blocks, f32),),
            2,
            ((row_blocks + 1, f32),),
            1,
            flops,
        )(plan, tile if first else flipped, x_bar)
        token = ()
        if first:
            after = own_image
        if direct:
            image = [partner(image[m - 1], m) for m in range(1, half)]
            kept = 1 if last else 2
            total, sent = call(near_sum_kernel, (shape(2 * span, f32), shape(kept * span, bf16)), 1 + half)(
                duals, own_image, *image
            )
            args = (duals, total, partner(sent, half))
            after = total
        if first:
            flipped, *token = pl.pallas_call(
                flip_kernel,
                out_shape=(pltpu.VMEM(blocks.shape, blocks.dtype), jax.ShapeDtypeStruct((8, BS), f32)),
                in_specs=[VMEM] * 2,
                out_specs=(VMEM,) * 2,
                compiler_params=PARAMS,
                cost_estimate=pl.CostEstimate(flops=16 * flops, bytes_accessed=0, transcendentals=0),
                name="flip_kernel",
            )(after, tile)
        if direct:
            if last:
                (y,) = call(last_dual_kernel, (jax.ShapeDtypeStruct((scen, span, BS), f32),), 4)(*args, y)
            else:
                y_own, y_far = (duals, y_half) if first else (y, y)
                y, y_half = call(dual_kernel, (shape(2 * span, f32), shape(2 * span, bf16)), 5 + len(token))(
                    *args, y_own, y_far, *token
                )
        else:
            image = lax.psum_scatter(own_image, "col", scatter_dimension=0, tiled=True)
            y, y_half = call(whole_dual_kernel, (shape(span, f32), shape(span, bf16)), 3)(
                duals[:span] if first else y, duals[span:], image
            )

    y = y if direct else jnp.transpose(y, (1, 0, 2))
    return (x[0].reshape(scen, 1, -1), y.reshape(scen, 1, -1))


def solution(mesh):
    return jax.shard_map(
        per_device,
        mesh=mesh,
        in_specs=(
            P("grp", "col", "row"),
            P("grp", "row", "col"),
            P("grp", "col", "row"),
            P("grp", "row", "col"),
            P(("grp", "col"), "row"),
            P(("grp", "col"), "row"),
            P(("grp", "col"), "row", None, None, None),
            P(("grp", "col"), "row", None),
            P(("grp", "col"), "row", None),
            P(("grp", "col"), "row"),
        ),
        out_specs=(P("grp", "col", "row"), P("grp", "row", "col")),
        check_vma=False,
    )
```

```python
import functools

import jax
import jax.numpy as jnp
from jax import lax
from jax.experimental import pallas as pl
from jax.experimental.pallas import tpu as pltpu
from jax.sharding import PartitionSpec as P

BS = 128
ITERS = 6
OWN, HERE, THERE = range(3)
WIDE, NARROW = (48, 56, 56), 16
NN = (((1,), (0,)), ((), ()))
NT = (((1,), (1,)), ((), ()))

SMEM = pl.BlockSpec(memory_space=pltpu.SMEM)
VMEM = pl.BlockSpec(memory_space=pltpu.VMEM)
HBM = pl.BlockSpec(memory_space=pltpu.HBM)
PARAMS = pltpu.CompilerParams(vmem_limit_bytes=24 * 2**20)


class Plan:
    def __init__(self, ref, slots, columns):
        self.ref = ref
        self.pairs, self.room = plan_size(slots, columns)

    def first(self, which):
        return self.ref[which - 1] if which else 0

    def runs(self, which):
        return self.ref[2 + 2 * which], self.ref[3 + 2 * which]

    def slot(self, i):
        return 8 + i

    def row(self, i):
        return 8 + 2 * self.room + i

    def col(self, pair):
        return 8 + 4 * self.room + pair


def plan_size(slots, columns):
    pairs = -(-(slots + 2 * columns) // (2 * NARROW)) * NARROW + sum(WIDE)
    return pairs, pairs + -(-slots // 2)


def setup_kernel(direct, half, count, *refs):
    given, (state, duals, y_half, order), held, sems = refs[:8], refs[8:12], refs[12:20], refs[20]
    copies = [pltpu.make_async_copy(a, b, sems.at[i]) for i, (a, b) in enumerate(zip(given, held))]
    for copy in copies:
        copy.start()
    for copy in copies:
        copy.wait()
    primal, cost, upper, kind, dual, rhs, brow, bcol = held
    cols, span, scen = state.shape[0], dual.shape[1], dual.shape[0]
    for b in range(cols):
        state[b, pl.ds(0, scen)] = primal[:, b, :]
        state[b, pl.ds(scen, scen)] = cost[:, b, :]
        state[b, pl.ds(2 * scen, 1)] = upper[pl.ds(b, 1)]
        state[b, pl.ds(2 * scen + 1, 1)] = kind[pl.ds(b, 1)].astype(jnp.float32)
    for b in range(span):
        y = dual[:, b, :]
        duals[b] = y
        duals[span + b] = rhs[:, b, :]
        y_half[b] = y.astype(y_half.dtype)
    columns = 2 * cols
    key = bcol[...] ^ (lax.axis_index("row") * cols)
    row = brow[...]
    if direct:
        row = row ^ (lax.axis_index("col") * span)
        key = key + jnp.where((row & ((half - 1) * span)) == 0, 0, columns)
    lanes = key.shape[1]
    slot = lanes * lax.broadcasted_iota(jnp.int32, key.shape, 0) + lax.broadcasted_iota(jnp.int32, key.shape, 1)
    order[pl.ds(0, key.shape[0])] = jnp.where(slot < count[0, 0], key, 2 * columns)
    order[pl.ds(key.shape[0], key.shape[0])] = row


def runs_of(count, step, run=16):
    def body(i, _):
        for k in range(run):
            step(i * run + k)
        return 0

    lax.fori_loop(0, count // run, body, 0)


def prepare_kernel(columns, rows, order, blocks, plan_ref, tile, keys, ends, sem, key_sems):
    copy = pltpu.make_async_copy(blocks, tile, sem)
    copy.start()
    key_copies = [
        pltpu.make_async_copy(order.at[i], keys.at[pl.ds(i * BS, BS)], key_sems.at[i]) for i in range(order.shape[0])
    ]
    for key_copy in key_copies:
        key_copy.start()
    slots = blocks.shape[0]
    plan = Plan(plan_ref, slots, columns)

    def clear(i, _):
        for k in range(2):
            plan_ref[plan.slot(2 * i + k)] = 0
            plan_ref[plan.row(2 * i + k)] = rows
        plan_ref[plan.col(i)] = 0
        return 0

    lax.fori_loop(0, plan.pairs, clear, 0, unroll=16)
    for c in range(2 * columns):
        ends[c] = 0
    for key_copy in key_copies:
        key_copy.wait()

    def tally(n):
        key = keys[n]
        ends[key] = ends[key] + 1

    ends[2 * columns] = 0
    runs_of(slots, tally)

    start = jnp.int32(0)
    half = columns // 2
    for which, keys_of in enumerate((range(columns), range(columns, columns + half), range(columns + half, 2 * columns))):
        first = start
        if which:
            plan_ref[which - 1] = first // 2
        for c in keys_of:
            size = ends[c]
            ends[c] = start
            start = start + ((size + 1) // 2) * 2
        pairs = (start - first) // 2
        wide = (pairs + WIDE[which] - 1 - 2 * NARROW) // WIDE[which]
        narrow = (jnp.maximum(pairs - wide * WIDE[which], 0) + NARROW - 1) // NARROW
        plan_ref[2 + 2 * which] = wide
        plan_ref[3 + 2 * which] = narrow
        start = first + 2 * (wide * WIDE[which] + narrow * NARROW)
    ends[2 * columns] = 2 * plan.pairs

    def put(n):
        key = keys[n]
        at = ends[key]
        ends[key] = at + 1
        plan_ref[plan.slot(at)] = n
        plan_ref[plan.row(at)] = keys[slots + n]
        plan_ref[plan.col(at // 2)] = lax.rem(key, columns)

    runs_of(slots, put)
    copy.wait()


def over_pairs(plan, which, step):
    begin, (wide, narrow) = plan.first(which), plan.runs(which)

    def run(i, _, size, start):
        step(start + i * size, size)
        return 0

    lax.fori_loop(0, wide, functools.partial(run, size=WIDE[which], start=begin), 0)
    begin = begin + wide * WIDE[which]
    lax.fori_loop(0, narrow, functools.partial(run, size=NARROW, start=begin), 0)


def transposed_products(plan, which, tile, vecs, acc, base=0):
    ref = plan.ref

    def step(first, n):
        terms = []
        for u in range(n):
            i = 2 * (first + u)
            left = [vecs[ref[plan.row(i + k)]] for k in range(2)]
            right = [tile[ref[plan.slot(i + k)]] for k in range(2)]
            terms.append(
                lax.dot_general(
                    jnp.concatenate(left, axis=1), jnp.concatenate(right, axis=0), NN, preferred_element_type=jnp.float32
                )
            )
        for u in range(n):
            acc[jnp.maximum(ref[plan.col(first + u)] - base, 0)] += terms[u]

    over_pairs(plan, which, step)


def products(plan, which, tile, flipped, vecs, acc, base=0):
    ref = plan.ref
    axis, dims = (1, NN) if flipped else (0, NT)

    def step(first, n):
        terms = []
        for u in range(n):
            i = 2 * (first + u)
            right = [tile[ref[plan.slot(i + k)]] for k in range(2)]
            terms.append(
                lax.dot_general(
                    vecs[jnp.maximum(ref[plan.col(first + u)] - base, 0)],
                    jnp.concatenate(right, axis=axis),
                    dims,
                    preferred_element_type=jnp.float32,
                )
            )
        for u in range(n):
            for k in range(2):
                acc[ref[plan.row(2 * (first + u) + k)]] += terms[u][:, k * BS : (k + 1) * BS]

    over_pairs(plan, which, step)


def backward_own_kernel(plan_ref, tile, piece, grad, vecs):
    plan = Plan(plan_ref, tile.shape[0], grad.shape[0])
    span = piece.shape[0] // 2
    rows = vecs.shape[0] - 1
    vecs[pl.ds(0, span)] = piece[pl.ds(0, span)]
    vecs[pl.ds(rows // 2, span)] = piece[pl.ds(span, span)]
    vecs[rows] = jnp.zeros(vecs.shape[1:], vecs.dtype)
    grad[...] = jnp.zeros(grad.shape, grad.dtype)
    transposed_products(plan, OWN, tile, vecs, grad)


def backward_there_kernel(plan_ref, tile, *refs):
    pieces, (begun, grad, vecs) = refs[:-3], refs[-3:]
    cols = grad.shape[0]
    half = len(pieces) + 1
    span = pieces[0].shape[0] // 2
    for m in range(1, half):
        vecs[pl.ds(m * span, span)] = pieces[m - 1][pl.ds(0, span)]
        vecs[pl.ds((m + half) * span, span)] = pieces[m - 1][pl.ds(span, span)]
    vecs[2 * half * span] = jnp.zeros(vecs.shape[1:], vecs.dtype)
    grad[...] = begun[pl.ds(cols, cols)]
    transposed_products(Plan(plan_ref, tile.shape[0], 2 * cols), THERE, tile, vecs, grad, cols)


def backward_here_kernel(plan_ref, tile, vecs, begun, grad):
    cols = grad.shape[0]
    grad[...] = begun[pl.ds(0, cols)]
    transposed_products(Plan(plan_ref, tile.shape[0], 2 * cols), HERE, tile, vecs, grad)


def primal_step(own, other, state, x_ref, x_out, x_bar):
    cols, scen = own.shape[:2]
    x = state[:, pl.ds(0, scen)] if x_ref is None else x_ref[...]
    cost = state[:, pl.ds(scen, scen)]
    upper, kind = state[:, pl.ds(2 * scen, 1)], state[:, pl.ds(2 * scen + 1, 1)]
    value = x - 0.4 * (cost - (own[...] + other[...]))
    lifted = jnp.where(kind == 2, value, jnp.maximum(value, 0.0))
    x_next = jnp.where(kind == 1, jnp.minimum(lifted, upper), lifted)
    x_bar[...] = (2.0 * x_next - x).astype(x_bar.dtype)
    return x_next


def forward_here_kernel(first, last, direct, plan_ref, tile, own, other, state, *refs):
    x_ref = None if first else refs[0]
    x_out, x_bar, acc = refs[-3:]
    x_next = primal_step(own, other, state, x_ref, x_out, x_bar)
    if last:
        for b in range(x_next.shape[0]):
            x_out[:, b, :] = x_next[b]
    else:
        x_out[...] = x_next
    if direct:
        acc[...] = jnp.zeros(acc.shape, acc.dtype)
        products(Plan(plan_ref, tile.shape[0], 2 * x_bar.shape[0]), HERE, tile, not first, x_bar, acc)


def forward_there_kernel(first, plan_ref, tile, own, other, begun, state, *refs):
    x_ref = None if first else refs[0]
    x_out, x_bar, *pieces, acc = refs if first else refs[1:]
    cols = x_bar.shape[0]
    x_out[...] = primal_step(own, other, state, x_ref, x_out, x_bar)
    if pieces:
        acc[...] = begun[...]
        products(Plan(plan_ref, tile.shape[0], 2 * cols), THERE, tile, not first, x_bar, acc, cols)
        half = len(pieces) + 1
        span = pieces[0].shape[0] // 2
        for m in range(1, half):
            for k, r in enumerate((m, m + half)):
                pieces[m - 1][pl.ds(k * span, span)] = acc[pl.ds(r * span, span)].astype(pieces[m - 1].dtype)


def forward_own_kernel(flipped, plan_ref, tile, here_bar, there_bar, piece, vecs, acc):
    cols = here_bar.shape[0]
    vecs[pl.ds(0, cols)] = here_bar[...]
    vecs[pl.ds(cols, cols)] = there_bar[...]
    acc[...] = jnp.zeros(acc.shape, acc.dtype)
    products(Plan(plan_ref, tile.shape[0], 2 * cols), OWN, tile, flipped, vecs, acc)
    span = piece.shape[0] // 2
    piece[pl.ds(0, span)] = acc[pl.ds(0, span)]
    piece[pl.ds(span, span)] = acc[pl.ds((acc.shape[0] - 1) // 2, span)]


def flip_kernel(after, tile, flipped, done):
    def run(i, _):
        for k in range(8):
            flipped[i * 8 + k] = tile[i * 8 + k].T
        return 0

    lax.fori_loop(0, tile.shape[0] // 8, run, 0)
    done[...] = jnp.zeros(done.shape, done.dtype)


def near_sum_kernel(duals, own, *refs):
    pieces, (total, sent) = refs[:-2], refs[-2:]
    image = own[...]
    for piece in pieces:
        image = image + piece[...].astype(jnp.float32)
    total[...] = image
    span = image.shape[0] // 2
    at = sent.shape[0] - span
    sent[pl.ds(at, span)] = image[span:].astype(sent.dtype)
    if at:
        sent[pl.ds(0, span)] = (image[:span] - duals[pl.ds(span, span)]).astype(sent.dtype)


def dual_kernel(duals, near, far, y_own, y_far, *refs):
    y_out, y_half = refs[-2:]
    span = near.shape[0] // 2
    here, there = pl.ds(0, span), pl.ds(span, span)
    own = y_own[here] + 0.9 * (duals[there] - (near[here] + far[there].astype(jnp.float32)))
    copy = y_far[there].astype(jnp.float32) - 0.9 * (far[here].astype(jnp.float32) + near[there])
    for at, y in ((here, jnp.maximum(0.0, own)), (there, jnp.maximum(0.0, copy))):
        y_out[at] = y
        y_half[at] = y.astype(y_half.dtype)


def last_dual_kernel(duals, near, far, y_own, y_out):
    span = far.shape[0]
    here, there = pl.ds(0, span), pl.ds(span, span)
    own = y_own[here] + 0.9 * (duals[there] - (near[here] + far[...].astype(jnp.float32)))
    y = jnp.maximum(0.0, own)
    for b in range(span):
        y_out[:, b, :] = y[b]


def whole_dual_kernel(y_ref, rhs, image, y_out, y_half):
    y = jnp.maximum(0.0, y_ref[...] + 0.9 * (rhs[...] - image[...]))
    y_out[...] = y
    y_half[...] = y.astype(y_half.dtype)


def in_blocks(a):
    return a.reshape(tuple(n for n in a.shape[:-1] if n > 1) + (-1, BS))


def per_device(
    cost, rhs, primal, dual, bound_kind, upper, kblocks, block_row, block_col, block_count
):
    n_col, n_row = lax.axis_size("col"), lax.axis_size("row")
    scen = primal.shape[0]
    span, cols = dual.shape[2] // BS, primal.shape[2] // BS
    row_blocks, col_blocks = span * n_col, cols * n_row
    direct = n_col in (4, 8) and span & (span - 1) == 0
    half = n_col // 2

    f32, bf16, i32 = jnp.float32, jnp.bfloat16, jnp.int32
    blocks = kblocks[0, 0]
    slots = blocks.shape[0]

    def swap(a):
        return lax.ppermute(a, "row", [(i, n_row - 1 - i) for i in range(n_row)])

    def partner(a, m):
        return lax.ppermute(a, "col", [(i, i ^ m) for i in range(n_col)])

    def near(a):
        return [partner(a, m) for m in range(1, half)]

    def shape(blocks, dtype):
        return jax.ShapeDtypeStruct((blocks, scen, BS), dtype)

    def call(kernel, outs, ins, scratch=(), scalars=0, flops=0):
        return pl.pallas_call(
            kernel,
            out_shape=outs,
            in_specs=[SMEM] * scalars + [VMEM] * ins,
            out_specs=tuple(VMEM for _ in outs),
            scratch_shapes=[pltpu.VMEM((blocks, scen, BS), dtype) for blocks, dtype in scratch],
            compiler_params=PARAMS,
            cost_estimate=pl.CostEstimate(flops=flops, bytes_accessed=0, transcendentals=0),
            name=getattr(kernel, "func", kernel).__name__,
        )

    given = [in_blocks(a) for a in (primal, cost, upper, bound_kind, dual, rhs, block_row, block_col)]
    state, duals, y_half, order = pl.pallas_call(
        functools.partial(setup_kernel, direct, half),
        out_shape=(
            jax.ShapeDtypeStruct((cols, 2 * scen + 2, BS), f32),
            shape(2 * span, f32),
            shape(span, bf16),
            jax.ShapeDtypeStruct((2 * slots // BS, BS), i32),
        ),
        in_specs=[SMEM] + [HBM] * 8,
        out_specs=(VMEM,) * 4,
        scratch_shapes=[pltpu.VMEM(a.shape, a.dtype) for a in given] + [pltpu.SemaphoreType.DMA((8,))],
        compiler_params=PARAMS,
        name="setup_kernel",
    )(block_count, *[pltpu.with_memory_space_constraint(a, pltpu.HBM) for a in given])
    other_state = swap(state)
    if direct:
        y_half, order = lax.optimization_barrier((jnp.concatenate([y_half, partner(y_half, half)]), order))
    plan, tile = pl.pallas_call(
        functools.partial(prepare_kernel, col_blocks, row_blocks),
        out_shape=(
            pltpu.SMEM((8 + 5 * plan_size(slots, col_blocks)[1],), i32),
            pltpu.VMEM(blocks.shape, blocks.dtype),
        ),
        in_specs=[VMEM, HBM],
        out_specs=(SMEM, VMEM),
        scratch_shapes=[
            pltpu.SMEM((order.size,), i32),
            pltpu.SMEM((2 * col_blocks + 1,), i32),
            pltpu.SemaphoreType.DMA,
            pltpu.SemaphoreType.DMA((order.shape[0],)),
        ],
        compiler_params=PARAMS,
        name="prepare_kernel",
    )(order, pltpu.with_memory_space_constraint(blocks, pltpu.HBM))

    flops = 2 * slots * BS * BS * scen
    backward_own = call(backward_own_kernel, (shape(col_blocks, f32),), 2, ((row_blocks + 1, bf16),), 1, flops)
    near_pieces = (shape(2 * span, bf16),) * (half - 1) if direct else ()
    x_here, x_there = (), ()
    half_shape, x_bar_shape = shape(cols, f32), shape(cols, bf16)
    for step in range(ITERS):
        first, last = step == 0, step == ITERS - 1
        blocks_now = tile if first else flipped
        if direct:
            y_near = near(y_half)
            (grad,) = backward_own(plan, tile, y_half)
            there, vecs = call(
                backward_there_kernel, (half_shape, shape(row_blocks + 1, bf16)), 1 + half, (), 1, flops
            )(plan, tile, *y_near, grad)
            (here,) = call(backward_here_kernel, (half_shape,), 3, (), 1, flops)(plan, tile, vecs, grad)
        else:
            (grad,) = backward_own(plan, tile, lax.all_gather(y_half, "col", axis=0, tiled=True))
            here, there = grad[:cols], grad[cols:]
        from_there, from_here = swap(there), swap(here)
        x_shape = jax.ShapeDtypeStruct((scen, cols, BS), f32) if last else half_shape
        x, here_bar, begun = call(
            functools.partial(forward_here_kernel, first, last, direct),
            (x_shape, x_bar_shape, shape(row_blocks + 1, f32)),
            4 if first else 5,
            (),
            1,
            flops,
        )(plan, blocks_now, here, from_there, state, *x_here)
        x_here = (x,)
        x, there_bar, *image = call(
            functools.partial(forward_there_kernel, first),
            (half_shape, x_bar_shape) + near_pieces,
            5 if first else 6,
            ((row_blocks + 1, f32),),
            1,
            flops,
        )(plan, blocks_now, there, from_here, begun, other_state, *x_there)
        x_there = (x,)
        (own_image,) = call(
            functools.partial(forward_own_kernel, not first),
            (shape(2 * span if direct else row_blocks, f32),),
            3,
            ((col_blocks, bf16), (row_blocks + 1, f32)),
            1,
            flops,
        )(plan, blocks_now, here_bar, there_bar)
        token = ()
        if first:
            after = own_image
        if direct:
            image = [partner(image[m - 1], m) for m in range(1, half)]
            kept = 1 if last else 2
            total, sent = call(near_sum_kernel, (shape(2 * span, f32), shape(kept * span, bf16)), 1 + half)(
                duals, own_image, *image
            )
            args = (duals, total, partner(sent, half))
            after = total
        if first:
            flipped, *token = pl.pallas_call(
                flip_kernel,
                out_shape=(pltpu.VMEM(blocks.shape, blocks.dtype), jax.ShapeDtypeStruct((8, BS), f32)),
                in_specs=[VMEM] * 2,
                out_specs=(VMEM,) * 2,
                compiler_params=PARAMS,
                cost_estimate=pl.CostEstimate(flops=16 * flops, bytes_accessed=0, transcendentals=0),
                name="flip_kernel",
            )(after, tile)
        if direct:
            if last:
                (y,) = call(last_dual_kernel, (jax.ShapeDtypeStruct((scen, span, BS), f32),), 4)(*args, y)
            else:
                y_own, y_far = (duals, y_half) if first else (y, y)
                y, y_half = call(dual_kernel, (shape(2 * span, f32), shape(2 * span, bf16)), 5 + len(token))(
                    *args, y_own, y_far, *token
                )
        else:
            image = lax.psum_scatter(own_image, "col", scatter_dimension=0, tiled=True)
            y, y_half = call(whole_dual_kernel, (shape(span, f32), shape(span, bf16)), 3)(
                duals[:span] if first else y, duals[span:], image
            )

    y = y if direct else jnp.transpose(y, (1, 0, 2))
    return (x_here[0].reshape(scen, 1, -1), y.reshape(scen, 1, -1))


def solution(mesh):
    return jax.shard_map(
        per_device,
        mesh=mesh,
        in_specs=(
            P("grp", "col", "row"),
            P("grp", "row", "col"),
            P("grp", "col", "row"),
            P("grp", "row", "col"),
            P(("grp", "col"), "row"),
            P(("grp", "col"), "row"),
            P(("grp", "col"), "row", None, None, None),
            P(("grp", "col"), "row", None),
            P(("grp", "col"), "row", None),
            P(("grp", "col"), "row"),
        ),
        out_specs=(P("grp", "col", "row"), P("grp", "row", "col")),
        check_vma=False,
    )
```

```python
import functools

import jax
import jax.numpy as jnp
from jax import lax
from jax.experimental import pallas as pl
from jax.experimental.pallas import tpu as pltpu
from jax.sharding import PartitionSpec as P

BS = 128
ITERS = 6
OWN, HERE, THERE = range(3)
WIDE, NARROW = (32, 56, 56), 8
NN = (((1,), (0,)), ((), ()))
NT = (((1,), (1,)), ((), ()))

SMEM = pl.BlockSpec(memory_space=pltpu.SMEM)
VMEM = pl.BlockSpec(memory_space=pltpu.VMEM)
HBM = pl.BlockSpec(memory_space=pltpu.HBM)
PARAMS = pltpu.CompilerParams(vmem_limit_bytes=24 * 2**20)


class Plan:
    def __init__(self, ref, slots, columns):
        self.ref = ref
        self.pairs, self.room = plan_size(slots, columns)

    def first(self, which):
        return self.ref[which - 1] if which else 0

    def runs(self, which):
        return self.ref[2 + 2 * which], self.ref[3 + 2 * which]

    def slot(self, i):
        return 8 + i

    def row(self, i):
        return 8 + 2 * self.room + i

    def col(self, pair):
        return 8 + 4 * self.room + pair


def plan_size(slots, columns):
    pairs = -(-(slots + 2 * columns) // (2 * NARROW)) * NARROW + sum(WIDE)
    return pairs, pairs + -(-slots // 2)


def setup_kernel(direct, half, count, *refs):
    given, (state, duals, y_half, order), held, sems = refs[:8], refs[8:12], refs[12:20], refs[20]
    copies = [pltpu.make_async_copy(a, b, sems.at[i]) for i, (a, b) in enumerate(zip(given, held))]
    for copy in copies:
        copy.start()
    for copy in copies:
        copy.wait()
    primal, cost, upper, kind, dual, rhs, brow, bcol = held
    cols, span, scen = state.shape[0], dual.shape[1], dual.shape[0]
    for b in range(cols):
        state[b, pl.ds(0, scen)] = primal[:, b, :]
        state[b, pl.ds(scen, scen)] = cost[:, b, :]
        state[b, pl.ds(2 * scen, 1)] = upper[pl.ds(b, 1)]
        state[b, pl.ds(2 * scen + 1, 1)] = kind[pl.ds(b, 1)].astype(jnp.float32)
    for b in range(span):
        y = dual[:, b, :]
        duals[b] = y
        duals[span + b] = rhs[:, b, :]
        y_half[b] = y.astype(y_half.dtype)
    columns = 2 * cols
    key = bcol[...] ^ (lax.axis_index("row") * cols)
    row = brow[...]
    if direct:
        row = row ^ (lax.axis_index("col") * span)
        key = key + jnp.where((row & ((half - 1) * span)) == 0, 0, columns)
    lanes = key.shape[1]
    slot = lanes * lax.broadcasted_iota(jnp.int32, key.shape, 0) + lax.broadcasted_iota(jnp.int32, key.shape, 1)
    order[pl.ds(0, key.shape[0])] = jnp.where(slot < count[0, 0], key, 2 * columns)
    order[pl.ds(key.shape[0], key.shape[0])] = row


def runs_of(count, step, run=16):
    def body(i, _):
        for k in range(run):
            step(i * run + k)
        return 0

    lax.fori_loop(0, count // run, body, 0)


def prepare_kernel(columns, rows, order, blocks, plan_ref, tile, keys, ends, sem, key_sems):
    copy = pltpu.make_async_copy(blocks, tile, sem)
    copy.start()
    key_copies = [
        pltpu.make_async_copy(order.at[i], keys.at[pl.ds(i * BS, BS)], key_sems.at[i]) for i in range(order.shape[0])
    ]
    for key_copy in key_copies:
        key_copy.start()
    slots = blocks.shape[0]
    plan = Plan(plan_ref, slots, columns)

    def clear(i, _):
        for k in range(2):
            plan_ref[plan.slot(2 * i + k)] = 0
            plan_ref[plan.row(2 * i + k)] = rows
        plan_ref[plan.col(i)] = 0
        return 0

    lax.fori_loop(0, plan.pairs, clear, 0, unroll=16)
    for c in range(2 * columns):
        ends[c] = 0
    for key_copy in key_copies:
        key_copy.wait()

    def tally(n):
        key = keys[n]
        ends[key] = ends[key] + 1

    ends[2 * columns] = 0
    runs_of(slots, tally)

    start = jnp.int32(0)
    half = columns // 2
    for which, keys_of in enumerate((range(columns), range(columns, columns + half), range(columns + half, 2 * columns))):
        first = start
        if which:
            plan_ref[which - 1] = first // 2
        for c in keys_of:
            size = ends[c]
            ends[c] = start
            start = start + ((size + 1) // 2) * 2
        pairs = (start - first) // 2
        wide = (pairs + WIDE[which] - 1 - 2 * NARROW) // WIDE[which]
        narrow = (jnp.maximum(pairs - wide * WIDE[which], 0) + NARROW - 1) // NARROW
        plan_ref[2 + 2 * which] = wide
        plan_ref[3 + 2 * which] = narrow
        start = first + 2 * (wide * WIDE[which] + narrow * NARROW)
    ends[2 * columns] = 2 * plan.pairs

    def put(n):
        key = keys[n]
        at = ends[key]
        ends[key] = at + 1
        plan_ref[plan.slot(at)] = n
        plan_ref[plan.row(at)] = keys[slots + n]
        plan_ref[plan.col(at // 2)] = lax.rem(key, columns)

    runs_of(slots, put)
    copy.wait()


def over_pairs(plan, which, step):
    begin, (wide, narrow) = plan.first(which), plan.runs(which)

    def run(i, _, size, start):
        step(start + i * size, size)
        return 0

    lax.fori_loop(0, wide, functools.partial(run, size=WIDE[which], start=begin), 0)
    begin = begin + wide * WIDE[which]
    lax.fori_loop(0, narrow, functools.partial(run, size=NARROW, start=begin), 0)


def transposed_products(plan, which, tile, vecs, acc, base=0):
    ref = plan.ref

    def step(first, n):
        terms = []
        for u in range(n):
            i = 2 * (first + u)
            left = [vecs[ref[plan.row(i + k)]] for k in range(2)]
            right = [tile[ref[plan.slot(i + k)]] for k in range(2)]
            terms.append(
                lax.dot_general(
                    jnp.concatenate(left, axis=1), jnp.concatenate(right, axis=0), NN, preferred_element_type=jnp.float32
                )
            )
        for u in range(n):
            acc[jnp.maximum(ref[plan.col(first + u)] - base, 0)] += terms[u]

    over_pairs(plan, which, step)


def products(plan, which, tile, flipped, vecs, acc, base=0):
    ref = plan.ref
    axis, dims = (1, NN) if flipped else (0, NT)

    def step(first, n):
        terms = []
        for u in range(n):
            i = 2 * (first + u)
            right = [tile[ref[plan.slot(i + k)]] for k in range(2)]
            terms.append(
                lax.dot_general(
                    vecs[jnp.maximum(ref[plan.col(first + u)] - base, 0)],
                    jnp.concatenate(right, axis=axis),
                    dims,
                    preferred_element_type=jnp.float32,
                )
            )
        for u in range(n):
            for k in range(2):
                acc[ref[plan.row(2 * (first + u) + k)]] += terms[u][:, k * BS : (k + 1) * BS]

    over_pairs(plan, which, step)


def backward_own_kernel(plan_ref, tile, piece, grad, vecs):
    plan = Plan(plan_ref, tile.shape[0], grad.shape[0])
    span = piece.shape[0] // 2
    rows = vecs.shape[0] - 1
    vecs[pl.ds(0, span)] = piece[pl.ds(0, span)]
    vecs[pl.ds(rows // 2, span)] = piece[pl.ds(span, span)]
    vecs[rows] = jnp.zeros(vecs.shape[1:], vecs.dtype)
    grad[...] = jnp.zeros(grad.shape, grad.dtype)
    transposed_products(plan, OWN, tile, vecs, grad)


def backward_there_kernel(plan_ref, tile, *refs):
    pieces, (begun, grad, vecs) = refs[:-3], refs[-3:]
    cols = grad.shape[0]
    half = len(pieces) + 1
    span = pieces[0].shape[0] // 2
    for m in range(1, half):
        vecs[pl.ds(m * span, span)] = pieces[m - 1][pl.ds(0, span)]
        vecs[pl.ds((m + half) * span, span)] = pieces[m - 1][pl.ds(span, span)]
    vecs[2 * half * span] = jnp.zeros(vecs.shape[1:], vecs.dtype)
    grad[...] = begun[pl.ds(cols, cols)]
    transposed_products(Plan(plan_ref, tile.shape[0], 2 * cols), THERE, tile, vecs, grad, cols)


def backward_here_kernel(plan_ref, tile, vecs, begun, grad):
    cols = grad.shape[0]
    grad[...] = begun[pl.ds(0, cols)]
    transposed_products(Plan(plan_ref, tile.shape[0], 2 * cols), HERE, tile, vecs, grad)


def primal_step(own, other, state, x_ref, x_out, x_bar):
    cols, scen = own.shape[:2]
    x = state[:, pl.ds(0, scen)] if x_ref is None else x_ref[...]
    cost = state[:, pl.ds(scen, scen)]
    upper, kind = state[:, pl.ds(2 * scen, 1)], state[:, pl.ds(2 * scen + 1, 1)]
    value = x - 0.4 * (cost - (own[...] + other[...]))
    lifted = jnp.where(kind == 2, value, jnp.maximum(value, 0.0))
    x_next = jnp.where(kind == 1, jnp.minimum(lifted, upper), lifted)
    x_bar[...] = (2.0 * x_next - x).astype(x_bar.dtype)
    return x_next


def forward_here_kernel(first, last, direct, plan_ref, tile, own, other, state, *refs):
    x_ref = None if first else refs[0]
    x_out, x_bar, acc = refs[-3:]
    x_next = primal_step(own, other, state, x_ref, x_out, x_bar)
    if last:
        for b in range(x_next.shape[0]):
            x_out[:, b, :] = x_next[b]
    else:
        x_out[...] = x_next
    if direct:
        acc[...] = jnp.zeros(acc.shape, acc.dtype)
        products(Plan(plan_ref, tile.shape[0], 2 * x_bar.shape[0]), HERE, tile, not first, x_bar, acc)


def forward_there_kernel(first, plan_ref, tile, own, other, begun, state, *refs):
    x_ref = None if first else refs[0]
    x_out, x_bar, *pieces, acc = refs if first else refs[1:]
    cols = x_bar.shape[0]
    x_out[...] = primal_step(own, other, state, x_ref, x_out, x_bar)
    if pieces:
        acc[...] = begun[...]
        products(Plan(plan_ref, tile.shape[0], 2 * cols), THERE, tile, not first, x_bar, acc, cols)
        half = len(pieces) + 1
        span = pieces[0].shape[0] // 2
        for m in range(1, half):
            for k, r in enumerate((m, m + half)):
                pieces[m - 1][pl.ds(k * span, span)] = acc[pl.ds(r * span, span)].astype(pieces[m - 1].dtype)


def forward_own_kernel(flipped, plan_ref, tile, here_bar, there_bar, piece, vecs, acc):
    cols = here_bar.shape[0]
    vecs[pl.ds(0, cols)] = here_bar[...]
    vecs[pl.ds(cols, cols)] = there_bar[...]
    acc[...] = jnp.zeros(acc.shape, acc.dtype)
    products(Plan(plan_ref, tile.shape[0], 2 * cols), OWN, tile, flipped, vecs, acc)
    span = piece.shape[0] // 2
    piece[pl.ds(0, span)] = acc[pl.ds(0, span)]
    piece[pl.ds(span, span)] = acc[pl.ds((acc.shape[0] - 1) // 2, span)]


def flip_kernel(after, tile, flipped, done):
    def run(i, _):
        for k in range(8):
            flipped[i * 8 + k] = tile[i * 8 + k].T
        return 0

    lax.fori_loop(0, tile.shape[0] // 8, run, 0)
    done[...] = jnp.zeros(done.shape, done.dtype)


def near_sum_kernel(duals, own, *refs):
    pieces, (total, sent) = refs[:-2], refs[-2:]
    image = own[...]
    for piece in pieces:
        image = image + piece[...].astype(jnp.float32)
    total[...] = image
    span = image.shape[0] // 2
    at = sent.shape[0] - span
    sent[pl.ds(at, span)] = image[span:].astype(sent.dtype)
    if at:
        sent[pl.ds(0, span)] = (image[:span] - duals[pl.ds(span, span)]).astype(sent.dtype)


def dual_kernel(duals, near, far, y_own, y_far, *refs):
    y_out, y_half = refs[-2:]
    span = near.shape[0] // 2
    here, there = pl.ds(0, span), pl.ds(span, span)
    own = y_own[here] + 0.9 * (duals[there] - (near[here] + far[there].astype(jnp.float32)))
    copy = y_far[there].astype(jnp.float32) - 0.9 * (far[here].astype(jnp.float32) + near[there])
    for at, y in ((here, jnp.maximum(0.0, own)), (there, jnp.maximum(0.0, copy))):
        y_out[at] = y
        y_half[at] = y.astype(y_half.dtype)


def last_dual_kernel(duals, near, far, y_own, y_out):
    span = far.shape[0]
    here, there = pl.ds(0, span), pl.ds(span, span)
    own = y_own[here] + 0.9 * (duals[there] - (near[here] + far[...].astype(jnp.float32)))
    y = jnp.maximum(0.0, own)
    for b in range(span):
        y_out[:, b, :] = y[b]


def whole_dual_kernel(y_ref, rhs, image, y_out, y_half):
    y = jnp.maximum(0.0, y_ref[...] + 0.9 * (rhs[...] - image[...]))
    y_out[...] = y
    y_half[...] = y.astype(y_half.dtype)


def in_blocks(a):
    return a.reshape(tuple(n for n in a.shape[:-1] if n > 1) + (-1, BS))


def per_device(
    cost, rhs, primal, dual, bound_kind, upper, kblocks, block_row, block_col, block_count
):
    n_col, n_row = lax.axis_size("col"), lax.axis_size("row")
    scen = primal.shape[0]
    span, cols = dual.shape[2] // BS, primal.shape[2] // BS
    row_blocks, col_blocks = span * n_col, cols * n_row
    direct = n_col in (4, 8) and span & (span - 1) == 0
    half = n_col // 2

    f32, bf16, i32 = jnp.float32, jnp.bfloat16, jnp.int32
    blocks = kblocks[0, 0]
    slots = blocks.shape[0]

    def swap(a):
        return lax.ppermute(a, "row", [(i, n_row - 1 - i) for i in range(n_row)])

    def partner(a, m):
        return lax.ppermute(a, "col", [(i, i ^ m) for i in range(n_col)])

    def near(a):
        return [partner(a, m) for m in range(1, half)]

    def shape(blocks, dtype):
        return jax.ShapeDtypeStruct((blocks, scen, BS), dtype)

    def call(kernel, outs, ins, scratch=(), scalars=0, flops=0):
        return pl.pallas_call(
            kernel,
            out_shape=outs,
            in_specs=[SMEM] * scalars + [VMEM] * ins,
            out_specs=tuple(VMEM for _ in outs),
            scratch_shapes=[pltpu.VMEM((blocks, scen, BS), dtype) for blocks, dtype in scratch],
            compiler_params=PARAMS,
            cost_estimate=pl.CostEstimate(flops=flops, bytes_accessed=0, transcendentals=0),
            name=getattr(kernel, "func", kernel).__name__,
        )

    given = [in_blocks(a) for a in (primal, cost, upper, bound_kind, dual, rhs, block_row, block_col)]
    state, duals, y_half, order = pl.pallas_call(
        functools.partial(setup_kernel, direct, half),
        out_shape=(
            jax.ShapeDtypeStruct((cols, 2 * scen + 2, BS), f32),
            shape(2 * span, f32),
            shape(span, bf16),
            jax.ShapeDtypeStruct((2 * slots // BS, BS), i32),
        ),
        in_specs=[SMEM] + [HBM] * 8,
        out_specs=(VMEM,) * 4,
        scratch_shapes=[pltpu.VMEM(a.shape, a.dtype) for a in given] + [pltpu.SemaphoreType.DMA((8,))],
        compiler_params=PARAMS,
        name="setup_kernel",
    )(block_count, *[pltpu.with_memory_space_constraint(a, pltpu.HBM) for a in given])
    other_state = swap(state)
    if direct:
        y_half, order = lax.optimization_barrier((jnp.concatenate([y_half, partner(y_half, half)]), order))
    plan, tile = pl.pallas_call(
        functools.partial(prepare_kernel, col_blocks, row_blocks),
        out_shape=(
            pltpu.SMEM((8 + 5 * plan_size(slots, col_blocks)[1],), i32),
            pltpu.VMEM(blocks.shape, blocks.dtype),
        ),
        in_specs=[VMEM, HBM],
        out_specs=(SMEM, VMEM),
        scratch_shapes=[
            pltpu.SMEM((order.size,), i32),
            pltpu.SMEM((2 * col_blocks + 1,), i32),
            pltpu.SemaphoreType.DMA,
            pltpu.SemaphoreType.DMA((order.shape[0],)),
        ],
        compiler_params=PARAMS,
        name="prepare_kernel",
    )(order, pltpu.with_memory_space_constraint(blocks, pltpu.HBM))

    flops = 2 * slots * BS * BS * scen
    backward_own = call(backward_own_kernel, (shape(col_blocks, f32),), 2, ((row_blocks + 1, bf16),), 1, flops)
    near_pieces = (shape(2 * span, bf16),) * (half - 1) if direct else ()
    x_here, x_there = (), ()
    half_shape, x_bar_shape = shape(cols, f32), shape(cols, bf16)
    for step in range(ITERS):
        first, last = step == 0, step == ITERS - 1
        blocks_now = tile if first else flipped
        if direct:
            y_near = near(y_half)
            (grad,) = backward_own(plan, tile, y_half)
            there, vecs = call(
                backward_there_kernel, (half_shape, shape(row_blocks + 1, bf16)), 1 + half, (), 1, flops
            )(plan, tile, *y_near, grad)
            (here,) = call(backward_here_kernel, (half_shape,), 3, (), 1, flops)(plan, tile, vecs, grad)
        else:
            (grad,) = backward_own(plan, tile, lax.all_gather(y_half, "col", axis=0, tiled=True))
            here, there = grad[:cols], grad[cols:]
        from_there, from_here = swap(there), swap(here)
        x_shape = jax.ShapeDtypeStruct((scen, cols, BS), f32) if last else half_shape
        x, here_bar, begun = call(
            functools.partial(forward_here_kernel, first, last, direct),
            (x_shape, x_bar_shape, shape(row_blocks + 1, f32)),
            4 if first else 5,
            (),
            1,
            flops,
        )(plan, blocks_now, here, from_there, state, *x_here)
        x_here = (x,)
        x, there_bar, *image = call(
            functools.partial(forward_there_kernel, first),
            (half_shape, x_bar_shape) + near_pieces,
            5 if first else 6,
            ((row_blocks + 1, f32),),
            1,
            flops,
        )(plan, blocks_now, there, from_here, begun, other_state, *x_there)
        x_there = (x,)
        (own_image,) = call(
            functools.partial(forward_own_kernel, not first),
            (shape(2 * span if direct else row_blocks, f32),),
            3,
            ((col_blocks, bf16), (row_blocks + 1, f32)),
            1,
            flops,
        )(plan, blocks_now, here_bar, there_bar)
        token = ()
        if first:
            after = own_image
        if direct:
            image = [partner(image[m - 1], m) for m in range(1, half)]
            kept = 1 if last else 2
            total, sent = call(near_sum_kernel, (shape(2 * span, f32), shape(kept * span, bf16)), 1 + half)(
                duals, own_image, *image
            )
            args = (duals, total, partner(sent, half))
            after = total
        if first:
            flipped, *token = pl.pallas_call(
                flip_kernel,
                out_shape=(pltpu.VMEM(blocks.shape, blocks.dtype), jax.ShapeDtypeStruct((8, BS), f32)),
                in_specs=[VMEM] * 2,
                out_specs=(VMEM,) * 2,
                compiler_params=PARAMS,
                cost_estimate=pl.CostEstimate(flops=16 * flops, bytes_accessed=0, transcendentals=0),
                name="flip_kernel",
            )(after, tile)
        if direct:
            if last:
                (y,) = call(last_dual_kernel, (jax.ShapeDtypeStruct((scen, span, BS), f32),), 4)(*args, y)
            else:
                y_own, y_far = (duals, y_half) if first else (y, y)
                y, y_half = call(dual_kernel, (shape(2 * span, f32), shape(2 * span, bf16)), 5 + len(token))(
                    *args, y_own, y_far, *token
                )
        else:
            image = lax.psum_scatter(own_image, "col", scatter_dimension=0, tiled=True)
            y, y_half = call(whole_dual_kernel, (shape(span, f32), shape(span, bf16)), 3)(
                duals[:span] if first else y, duals[span:], image
            )

    y = y if direct else jnp.transpose(y, (1, 0, 2))
    return (x_here[0].reshape(scen, 1, -1), y.reshape(scen, 1, -1))


def solution(mesh):
    return jax.shard_map(
        per_device,
        mesh=mesh,
        in_specs=(
            P("grp", "col", "row"),
            P("grp", "row", "col"),
            P("grp", "col", "row"),
            P("grp", "row", "col"),
            P(("grp", "col"), "row"),
            P(("grp", "col"), "row"),
            P(("grp", "col"), "row", None, None, None),
            P(("grp", "col"), "row", None),
            P(("grp", "col"), "row", None),
            P(("grp", "col"), "row"),
        ),
        out_specs=(P("grp", "col", "row"), P("grp", "row", "col")),
        check_vma=False,
    )
```
